256 devices in a mesh: band: 16 (over x, y), patch: 8 (over z), rep: 2 (over core).
Axes of the slice: x: 4, y: 4, z: 8, core: 2. Of those that a mesh axis runs over, the one named last changes fastest.
Arguments:
- grid_latents: bfloat16 [2, 65536, 512], P('rep', ('band', 'patch')), may hold values from -6 to 6
- mesh_latents: bfloat16 [2, 32768, 512], P('rep', ('band', 'patch')), may hold values from -6 to 6
- weights: bfloat16 [7, 512, 512], replicated, may hold values from -0.25 to 0.25
- target_band: int32 [512, 1], P(('band', 'patch')), may hold values from 0 to 15; in each aligned block of 4 rows (0 to 3, 4 to 7, ...) at most 2 rows name the same one
- target_block: int32 [512], P(('band', 'patch')), may hold values from 0 to 1
- node_slot: int32 [65536], P(('band', 'patch')), may hold values from 0 to 127
- neighbours: int32 [32768, 6], P(('band', 'patch')), may hold values from 0 to 32767, as said below
- mesh_cotangent: bfloat16 [2, 32768, 512], P('rep', ('band', 'patch')), may hold values from -6 to 6
Outputs:
- grid_grad: bfloat16 [2, 65536, 512], P('rep', ('band', 'patch'))
- mesh_grad: bfloat16 [2, 32768, 512], P('rep', ('band', 'patch'))
- weight_grads: float32 [7, 512, 512], P(None, 'band')
The draws below stay inside these ranges and needn't reach their ends.
Inputs may be any that keep to these rules, and one draw needn't show every extreme that they name: `target_band`: of the 4 grid blocks on one device, at most 2 name the same band, and that many do for some band on some device in every draw. `neighbours`: every neighbour of a mesh node is owned by the node's own device or by one of the two devices next to it in band-then-patch order, wrapping around.
All inputs are finite; a program needn't handle non-finite values.
Results may differ from the reference program's by a relative error of at most 0.022.
Values may be sent and summed in bfloat16 or wider, within the bound.
No kernel may reach another device: no remote copies, remote signals or barrier semaphores. Data moves between devices by JAX's collectives and lax.ppermute only.
A program may use at most 128 MiB of HBM per device.

```python
import math
import jax
import jax.numpy as jnp
import numpy as np
from jax import lax

L = 512
BLOCK = 128
K = 6
GB = 4
MB = 2
SAMPLES = 2
CAP = 2
NGB = 512
NG = 65536
NM = 32768
N_BAND = 16
N_PATCH = 8


def draw_neighbours(key, part):
    key = jax.random.fold_in(key, 7)
    first_key, second_key = jax.random.split(key)
    mesh_rows = MB * BLOCK
    device_count = NM // mesh_rows
    node = jnp.arange(NM, dtype=jnp.int32)[:, None]
    home = node // mesh_rows
    offset = jax.random.randint(first_key, (NM, K), -1, 2, dtype=jnp.int32)
    local_rows = jax.random.randint(second_key, (NM, K), 0, mesh_rows, dtype=jnp.int32)
    result = jnp.mod(home + offset, device_count) * mesh_rows + local_rows
    result = result.at[0, 0].set(NM - 1)
    result = result.at[NM - 1, 1].set(0)
    return result.astype(jnp.int32)


def place_ends(array, key, low, high):
    place = [jax.random.randint(jax.random.fold_in(key, axis), (), 0, length) for axis, length in enumerate(array.shape)]
    main_axis = array.shape.index(max(array.shape))
    neighbour = place[:main_axis] + [(place[main_axis] + 1) % array.shape[main_axis]] + place[main_axis + 1:]
    return array.at[tuple(place)].set(low).at[tuple(neighbour)].set(high)


def levels(rng, extent, pieces, low, high):
    level = 1.0
    for axis_at, blocks in pieces:
        heights = jax.random.uniform(jax.random.fold_in(jax.random.fold_in(rng, 6), axis_at), (blocks,), jnp.float32, low / len(pieces), high / len(pieces))
        level = level * jnp.repeat(jnp.exp(heights), extent[axis_at] // blocks).reshape((-1,) + (1,) * (len(extent) - 1 - axis_at))
    return level


def deal_out(own_key, own, number, rows, number_of, top, most, lean):
    sequence = jax.random.permutation(own_key, number_of)
    heavy_load, ordinary = load_shares(number_of, rows * top, most, lean, True), load_shares(number_of, rows * top, most, lean, False)
    places = jnp.arange(number_of)

    def named(tallies, offset_by):
        used = int((tallies > 0).sum())
        fixed = max(1, used // 4)
        shifted = fixed + (places - fixed + offset_by * (used - fixed)) % max(1, number_of - fixed)
        return jnp.zeros((number_of,), jnp.int32).at[sequence[jnp.where(places < fixed, places, shifted)]].set(jnp.asarray(tallies, jnp.int32))

    tallies = jnp.where(number % 4 == 0, named(heavy_load, number // 4), named(ordinary, number - number // 4 - 1))
    mixed = jax.random.permutation(jax.random.fold_in(own, 3), number_of)
    donor, taker = mixed[0:number_of // 2 * 2:2], mixed[1:number_of // 2 * 2:2]
    margin = jnp.minimum(tallies[donor] - 1, most - tallies[taker]) // 2
    margin = jnp.where((donor == sequence[0]) | (taker == sequence[0]) | (tallies[taker] == 0), 0, jnp.maximum(margin, 0))
    shifted = jax.random.randint(jax.random.fold_in(own, 4), (number_of // 2,), 0, 1 << 20) % (margin + 1)
    tallies = tallies.at[donor].add(-shifted).at[taker].add(shifted)
    members = jnp.searchsorted(jnp.cumsum(tallies), jnp.arange(rows * top), side="right").astype(jnp.int32)
    listing = members.reshape(top, rows).T
    listing = listing[jax.random.permutation(jax.random.fold_in(own, 1), rows)]
    offset_by = jax.random.randint(jax.random.fold_in(own, 2), (rows, 1), 0, top)
    return jnp.take_along_axis(listing, (jnp.arange(top)[None, :] + offset_by) % top, axis=1)


def load_shares(number_of, total, reach, slope, full):
    portions = [(1 << 20) // math.isqrt(rank ** slope) + 1 for rank in range(1, number_of + 1)]
    largest = reach if full else min(reach, max(-(-total // number_of), total * portions[0] // sum(portions)))
    least = 1 if total - largest >= number_of - 1 else 0
    given, rest = [largest] + [least] * (number_of - 1), total - largest - least * (number_of - 1)
    while rest > 0:
        movable = [i for i in range(1, number_of) if given[i] < largest] or [i for i in range(1, number_of) if given[i] < reach]
        mass, remaining = sum([portions[i] for i in movable]), rest
        for i in movable:
            addition = min(reach - given[i], max(1, remaining * portions[i] // mass), rest)
            given[i] = given[i] + addition
            rest = rest - addition
    return np.array(given)


def normal_values(own_key, dims, spread, limit, cuts=(), kind=jnp.bfloat16):
    factor_of = levels(own_key, dims, cuts, -0.22, 0.18) if cuts else 1.0
    array = jax.random.normal(own_key, dims, jnp.float32) * spread * factor_of
    return jnp.minimum(jnp.maximum(array, -limit), limit).astype(kind)


def setup_inputs(seed: int = 0) -> dict:
    splits = jax.random.split(jax.random.key(seed), 9)
    grid_latents = normal_values(splits[0], (SAMPLES, NG, L), 1.0, 6.0, ((0, 2), (1, 128)))
    mesh_latents = normal_values(splits[1], (SAMPLES, NM, L), 1.0, 6.0, ((0, 2), (1, 128)))
    weights = normal_values(splits[2], (7, L, L), L ** -0.5, 0.25)
    target_band_keys = jax.random.split(jax.random.fold_in(splits[3], 1), NGB // GB)
    target_band_turns = jax.random.permutation(jax.random.fold_in(splits[3], 3), NGB // GB)
    target_band = jax.vmap(lambda own, number: deal_out(jax.random.fold_in(splits[3], 2), own, number, GB, N_BAND, 1, CAP, 2))(target_band_keys, target_band_turns).reshape((NGB, 1))
    target_block = place_ends(jax.random.randint(splits[4], (NGB,), 0, MB), jax.random.fold_in(splits[4], 1), 0, MB - 1).astype(jnp.int32)
    node_slot = place_ends(jax.random.randint(splits[5], (NG,), 0, BLOCK), jax.random.fold_in(splits[5], 1), 0, BLOCK - 1).astype(jnp.int32)
    neighbours = draw_neighbours(jax.random.fold_in(splits[8], 71), 0)
    mesh_cotangent = normal_values(splits[7], (SAMPLES, NM, L), 1.0, 6.0, ((0, 2), (1, 128)))
    return dict(grid_latents=grid_latents, mesh_latents=mesh_latents, weights=weights, target_band=target_band, target_block=target_block, node_slot=node_slot, neighbours=neighbours, mesh_cotangent=mesh_cotangent)


def silu_slope(value):
    sigma = jax.nn.sigmoid(value)
    return sigma * (1.0 + value * (1.0 - sigma))

def matmul(left, right):
    return jnp.dot(left, right, preferred_element_type=jnp.float32)

def reference(grid_latents, mesh_latents, weights, target_band, target_block, node_slot, neighbours, mesh_cotangent):
    grid_blocks = jnp.arange(NGB).astype(jnp.int32)
    patch_of = grid_blocks // GB % N_PATCH
    owner_dev = target_band[:, 0] * N_PATCH + patch_of
    block_base = (owner_dev * MB + target_block) * BLOCK
    target = (jnp.repeat(block_base, BLOCK) + node_slot).astype(jnp.int32)
    grid_outs = []
    mesh_outs = []
    grad_totals = [jnp.zeros((L, L), jnp.float32) for column in range(7)]
    for sample in range(SAMPLES):
        inputs = grid_latents[sample]
        first_pre = matmul(inputs, weights[0])
        hidden = jax.nn.silu(first_pre).astype(jnp.bfloat16)
        message = matmul(hidden, weights[1]).astype(jnp.bfloat16)
        aggregate = jax.ops.segment_sum(message.astype(jnp.float32), target, num_segments=NM)
        aggregate_b = aggregate.astype(jnp.bfloat16)
        second = matmul(aggregate_b, weights[2])
        squashed = jax.nn.silu(second).astype(jnp.bfloat16)
        latent = mesh_latents[sample].astype(jnp.float32) + matmul(squashed, weights[3])
        latent_b = latent.astype(jnp.bfloat16)
        sender = matmul(latent_b, weights[4])
        receiver = matmul(latent_b, weights[5])
        summed = jnp.zeros((NM, L), jnp.float32)
        for column in range(K):
            pre_act = jnp.take(sender, neighbours[:, column], axis=0) + receiver
            summed = summed + jax.nn.silu(pre_act)
        summed_b = summed.astype(jnp.bfloat16)
        cotangent = mesh_cotangent[sample]
        grad_out_w = matmul(summed_b.T, cotangent)
        grad_summed = matmul(cotangent, weights[6].T)
        grad_recv = jnp.zeros((NM, L), jnp.float32)
        grad_send = jnp.zeros((NM, L), jnp.float32)
        for column in range(K):
            edge_rows = neighbours[:, column]
            pre_act = jnp.take(sender, edge_rows, axis=0) + receiver
            edge_grad = lax.optimization_barrier((grad_summed * silu_slope(pre_act)).astype(jnp.bfloat16)).astype(jnp.float32)
            grad_recv = grad_recv + edge_grad
            grad_send = grad_send + jax.ops.segment_sum(edge_grad, edge_rows, num_segments=NM)
        grad_send_b = grad_send.astype(jnp.bfloat16)
        grad_recv_b = grad_recv.astype(jnp.bfloat16)
        grad_ws = matmul(latent_b.T, grad_send_b)
        grad_wr = matmul(latent_b.T, grad_recv_b)
        grad_latent = cotangent.astype(jnp.float32) + matmul(grad_send_b, weights[4].T) + matmul(grad_recv_b, weights[5].T)
        grad_latent_b = grad_latent.astype(jnp.bfloat16)
        grad_wo = matmul(squashed.T, grad_latent_b)
        grad_squashed = matmul(grad_latent_b, weights[3].T)
        grad_second = (grad_squashed * silu_slope(second)).astype(jnp.bfloat16)
        grad_wa = matmul(aggregate_b.T, grad_second)
        grad_aggregate = matmul(grad_second, weights[2].T).astype(jnp.bfloat16)
        grad_message = jnp.take(grad_aggregate, target, axis=0)
        grad_w2 = matmul(hidden.T, grad_message)
        grad_hidden = matmul(grad_message, weights[1].T)
        grad_first = (grad_hidden * silu_slope(first_pre)).astype(jnp.bfloat16)
        grad_w1 = matmul(inputs.T, grad_first)
        grid_outs.append(matmul(grad_first, weights[0].T).astype(jnp.bfloat16))
        mesh_outs.append(grad_latent_b)
        terms = [grad_w1, grad_w2, grad_wa, grad_wo, grad_ws, grad_wr, grad_out_w]
        grad_totals = [grad_totals[column] + terms[column] for column in range(7)]
    grid_scale = 1.0 / jnp.sqrt(jnp.float32(SAMPLES * NG))
    mesh_scale = 1.0 / jnp.sqrt(jnp.float32(SAMPLES * NM))
    scaled = [grad_totals[0] * grid_scale, grad_totals[1] * grid_scale] + [grad_totals[column] * mesh_scale for column in range(2, 7)]
    return (jnp.stack(grid_outs), jnp.stack(mesh_outs), jnp.stack(scaled))
```

```python
import math

import jax
import jax.numpy as jnp
from jax import lax
from jax.experimental import pallas as pl
from jax.experimental.pallas import tpu as pltpu
from jax.sharding import PartitionSpec as P

F32 = jnp.float32
BF16 = jnp.bfloat16
I32 = jnp.int32
ALL = ("band", "patch", "rep")
NX, NY, NZ, NR = 4, 4, 8, 2
LAT = 512
BLK = 128
GB = 4
MESH = 256
K = 6
META = 16
VMEM = pl.BlockSpec(memory_space=pltpu.VMEM)
SMEM = pl.BlockSpec(memory_space=pltpu.SMEM)


def nn(a, b):
    return lax.dot_general(a, b, (((1,), (0,)), ((), ())), preferred_element_type=F32)


def nt(a, b):
    return lax.dot_general(a, b, (((1,), (1,)), ((), ())), preferred_element_type=F32)


def tn(a, b):
    return lax.dot_general(a, b, (((0,), (0,)), ((), ())), preferred_element_type=F32)


def sigmoid(v):
    return 0.5 * jnp.tanh(0.5 * v) + 0.5


def call(kernel, ins, outs, scratch=(), flops=0, limit=40):
    specs_in = [SMEM if s else VMEM for _, s in ins]
    out_shape = [jax.ShapeDtypeStruct(shape, dtype) for shape, dtype, _ in outs]
    specs_out = [SMEM if s else VMEM for _, _, s in outs]
    return pl.pallas_call(
        kernel,
        out_shape=out_shape,
        in_specs=specs_in,
        out_specs=specs_out,
        scratch_shapes=list(scratch),
        compiler_params=pltpu.CompilerParams(vmem_limit_bytes=limit * 1024 * 1024),
        cost_estimate=pl.CostEstimate(flops=flops, bytes_accessed=1000000, transcendentals=0),
    )(*[a for a, _ in ins])


def device(x, y, z, r):
    return ((x * NY + y) * NZ + z) * NR + r


def shifts(k, flip):
    pairs = []
    for x in range(NX):
        for y in range(NY):
            for z in range(NZ):
                for r in range(NR):
                    along_x = (r == 0) != flip
                    to = device((x + k) % NX, y, z, r) if along_x else device(x, (y + k) % NY, z, r)
                    pairs.append((device(x, y, z, r), to))
    return pairs


def first(v, k):
    return lax.ppermute(v, ALL, shifts(k, False))


def second(v, k):
    return lax.ppermute(v, ALL, shifts(k, True))


def split_code(code, rep):
    t = lax.shift_right_logical(code, 1)
    tx = lax.shift_right_logical(t, 2)
    ty = t & 3
    d1 = jnp.where(rep == 0, tx, ty)
    d2 = jnp.where(rep == 0, ty, tx)
    return d1, d2, code & 1


def grid_forward(codes, x, w, slot, out, slope):
    row = lax.broadcasted_iota(I32, (BLK, BLK), 0)
    for g in range(GB):
        rows = pl.ds(g * BLK, BLK)
        v = nn(x[rows, :], w[...])
        sg = sigmoid(v)
        h = v * sg
        slope[rows, :] = (sg + h * (1.0 - sg)).astype(BF16)
        pick = jnp.where(row == slot[g : g + 1, :], 1.0, 0.0).astype(BF16)
        out[rows, :] = nn(pick, h.astype(BF16)).astype(BF16)
    meta_row = lax.broadcasted_iota(I32, (META, LAT), 0)
    meta = jnp.zeros((META, LAT), F32)
    for g in range(GB):
        meta = jnp.where(meta_row == g, codes[g].astype(F32), meta)
    out[pl.ds(GB * BLK, META), :] = meta.astype(BF16)


def route_sum(pos, p0, p1, p2, p3, q0, q1, q2, q3, table, acc):
    acc[...] = jnp.zeros_like(acc)
    own1, own2, rep = pos[0], pos[1], pos[2]
    for j, p in enumerate((p0, p1, p2, p3)):
        meta = p[pl.ds(GB * BLK, META), :].astype(F32)
        for i in range(GB):
            code = jnp.max(meta[i : i + 1, 0:128]).astype(I32)
            table[j * GB + i] = code
            d1, d2, blk = split_code(code, rep)
            slot = ((d2 - own2) & 3) * 2 + blk

            @pl.when(d1 == own1)
            def _():
                acc[slot] += p[pl.ds(i * BLK, BLK), :].astype(F32)

    for k, q in enumerate((q0, q1, q2, q3)):
        for b in range(2):
            q[pl.ds(b * BLK, BLK), :] = acc[2 * k + b].astype(q.dtype)


def mesh_forward(q0, r1, r2, r3, ml, w1, w2, w3, ah, agg, sq, slope, lat):
    total = q0[...] + r1[...].astype(F32) + r2[...].astype(F32) + r3[...].astype(F32)
    ah[...] = total.astype(BF16)
    agg[...] = nn(ah[...], w1[...]).astype(BF16)
    v = nn(agg[...], w2[...])
    sg = sigmoid(v)
    s = v * sg
    slope[...] = (sg + s * (1.0 - sg)).astype(BF16)
    sq[...] = s.astype(BF16)
    lat[...] = (ml[...].astype(F32) + nn(sq[...], w3[...])).astype(BF16)


def own_tables(lat, w4, w5, snd, rcv):
    snd[...] = nn(lat[...], w4[...]).astype(BF16)
    rcv[...] = nn(lat[...], w5[...])


def cot_tables(cot, cp, cn, w6, gs):
    for j, c in enumerate((cp, cot, cn)):
        gs[pl.ds(j * MESH, MESH), :] = nt(c[pl.ds(0, MESH), :], w6[...])


def edges_backward(
    lp, ln, snd, rcv, col, row, cp, cn, gs, cot, slope2, w1, w2, w3, w4, w5,
    summed_b, gsend_b, grecv_b, gl_b, gsec_b, ga_b, gm_b,
    table, srcv, ecol, e, gsend,
):
    table[pl.ds(MESH, MESH), :] = snd[...]
    table[pl.ds(0, MESH), :] = nn(lp[...], w4[...]).astype(BF16)
    table[pl.ds(2 * MESH, MESH), :] = nn(ln[...], w4[...]).astype(BF16)
    srcv[pl.ds(0, MESH), :] = nn(lp[...], w5[...])
    srcv[pl.ds(MESH, MESH), :] = nn(ln[...], w5[...])
    half = 128
    lane = lax.broadcasted_iota(I32, (half, 3 * MESH), 1)
    for m in range(2):
        rows = pl.ds(m * half, half)
        total = jnp.zeros((half, LAT), F32)
        recv = jnp.zeros((half, LAT), F32)
        for k in range(K):
            pick = jnp.where(lane == col[rows, k : k + 1], 1.0, 0.0).astype(BF16)
            v = nn(pick, table[...]) + rcv[rows, :]
            sg = sigmoid(v)
            s = v * sg
            total = total + s
            eg = (gs[pl.ds(MESH + m * half, half), :] * (sg + s * (1.0 - sg))).astype(BF16)
            recv = recv + eg.astype(F32)
            e[pl.ds(k * MESH + m * half, half), :] = eg
        summed_b[rows, :] = total.astype(BF16)
        grecv_b[rows, :] = recv.astype(BF16)
    own = lax.broadcasted_iota(I32, (MESH, MESH), 0)
    acc = jnp.zeros((MESH, LAT), F32)
    for k in range(K):
        pick = jnp.where(own + MESH == row[k : k + 1, :], 1.0, 0.0).astype(BF16)
        acc = acc + nn(pick, e[pl.ds(k * MESH, MESH), :])
    gsend[...] = acc
    lane2 = lax.broadcasted_iota(I32, (half, MESH), 1).astype(F32)
    ownf = own.astype(F32)
    for side, c in enumerate((cp, cn)):
        codes = c[pl.ds(MESH, META), 0:MESH].astype(F32)
        ecol[...] = jnp.transpose(codes)
        for k in range(K):
            for m in range(2):
                rows = pl.ds(m * half, half)
                pick = jnp.where(lane2 == ecol[rows, k : k + 1], 1.0, 0.0).astype(BF16)
                v = nn(pick, table[pl.ds(MESH, MESH), :]) + srcv[pl.ds(side * MESH + m * half, half), :]
                sg = sigmoid(v)
                s = v * sg
                g = gs[pl.ds(2 * side * MESH + m * half, half), :]
                e[pl.ds(k * MESH + m * half, half), :] = (g * (sg + s * (1.0 - sg))).astype(BF16)
        acc = gsend[...]
        for k in range(K):
            pick = jnp.where(ownf == codes[k : k + 1, :], 1.0, 0.0).astype(BF16)
            acc = acc + nn(pick, e[pl.ds(k * MESH, MESH), :])
        gsend[...] = acc
    gsend_b[...] = gsend[...].astype(BF16)
    gl = cot[...].astype(F32) + nt(gsend_b[...], w4[...]) + nt(grecv_b[...], w5[...])
    gl_b[...] = gl.astype(BF16)
    gsec_b[...] = (nt(gl_b[...], w3[...]) * slope2[...].astype(F32)).astype(BF16)
    ga_b[...] = nt(gsec_b[...], w2[...]).astype(BF16)
    gm_b[...] = nt(ga_b[...], w1[...]).astype(BF16)


def mesh_weights(pos, ah, agg, sq, lat, summed, ga, gsec, gl, gsend, grecv, cot, keep, give):
    rep = pos[2]
    pairs = ((ah, ga), (agg, gsec), (sq, gl), (lat, gsend), (lat, grecv), (summed, cot))
    for w, (left, right) in enumerate(pairs):
        for out, h in ((keep, rep), (give, 1 - rep)):
            cols = pl.ds(pl.multiple_of(h * 256, 256), 256)
            part = tn(left[...], right[:, cols]).astype(BF16)
            for t in range(2):
                q, at = (2 * w + t) // 3, (2 * w + t) % 3
                for c in range(2):
                    for b in range(16):
                        out[c * 4 + q, pl.ds(b * 48 + at * 16, 16), :] = part[
                            b * 32 + t * 16 : b * 32 + t * 16 + 16, c * 128 : c * 128 + 128
                        ]


def return_pick(pos, table, g0, g1, g2, g3, r0, r1, r2, r3):
    own1, own2, rep = pos[0], pos[1], pos[2]
    sources = (g0, g1, g2, g3)
    for k, r in enumerate((r0, r1, r2, r3)):
        j = (4 - k) % 4
        for i in range(GB):
            d1, d2, blk = split_code(table[j * GB + i], rep)
            at = (own2 - d2) & 3
            for n in range(4):

                @pl.when((d1 == own1) & (at == n))
                def _():
                    start = pl.multiple_of(blk * BLK, BLK)
                    r[pl.ds(i * BLK, BLK), :] = sources[n][pl.ds(start, BLK), :]


def grid_backward(pos, codes, r0, r1, r2, r3, x, slot, slope, gf, part, picked):
    own1, rep = pos[0], pos[2]
    row = lax.broadcasted_iota(I32, (BLK, BLK), 0)
    for i in range(GB):
        d1, _, _ = split_code(codes[i], rep)
        at = (own1 - d1) & 3
        rows = pl.ds(i * BLK, BLK)
        for n, r in enumerate((r0, r1, r2, r3)):

            @pl.when(at == n)
            def _():
                picked[rows, :] = r[rows, :]

    for i in range(GB):
        rows = pl.ds(i * BLK, BLK)
        pick = jnp.where(row == slot[i : i + 1, :], 1.0, 0.0).astype(BF16)
        gf[rows, :] = (tn(pick, picked[rows, :]) * slope[rows, :].astype(F32)).astype(BF16)
    w = tn(x[...], gf[...]).astype(BF16)
    for b in range(16):
        for c in range(4):
            part[b, pl.ds(c * 32, 32), :] = w[b * 32 : b * 32 + 32, c * 128 : c * 128 + 128]


def grid_output(gf, w, out):
    out[...] = nt(gf[...], w[...]).astype(BF16)


def z_sum(parts, out):
    total = parts[0].astype(F32)
    for j in range(1, 8):
        total = total + parts[j].astype(F32)
    out[...] = total.astype(BF16)


def band_sum(parts, out):
    total = parts[0].astype(F32)
    for j in range(1, 16):
        total = total + parts[j].astype(F32)
    done = total.astype(BF16)
    for j in range(16):
        out[j] = done


def finish(parts, out, *, grid_scale, mesh_scale):
    total = parts[0, 0:128, :].astype(F32)
    for j in range(1, 16):
        total = total + parts[j, 0:128, :].astype(F32)
    total = total * grid_scale
    for c in range(4):
        out[0, :, pl.ds(c * 128, 128)] = total[c * 32 : c * 32 + 32, :]
    for z in range(8):
        c, q = z // 4, z % 4
        for r in range(2):
            piece = parts[z * 2 + r, 128:176, :].astype(F32)
            for t in range(3):
                n = q * 3 + t
                scale = grid_scale if n < 2 else mesh_scale
                out[1 + n // 2, pl.ds((n % 2) * 16, 16), pl.ds(r * 256 + c * 128, 128)] = (
                    piece[t * 16 : t * 16 + 16, :] * scale
                )


def body(
    grid_latents, mesh_latents, weights, target_band, target_block, node_slot, neighbours, mesh_cotangent
):
    grid_scale = 1.0 / math.sqrt(NR * GB * BLK * NX * NY * NZ)
    mesh_scale = 1.0 / math.sqrt(NR * MESH * NX * NY * NZ)
    band = lax.axis_index("band")
    patch = lax.axis_index("patch")
    rep = lax.axis_index("rep")
    bx, by = band // 4, band % 4
    pos = jnp.stack(
        [jnp.where(rep == 0, bx, by), jnp.where(rep == 0, by, bx), rep, patch]
    ).astype(I32)
    w = [weights[i] for i in range(7)]
    x = grid_latents[0]
    ml = mesh_latents[0]
    cot = mesh_cotangent[0]
    codes = target_band[:, 0] * 2 + target_block
    slot = node_slot.reshape(GB, BLK)

    p0, slope1 = call(
        grid_forward,
        [(codes, 1), (x, 0), (w[0], 0), (slot, 0)],
        [((GB * BLK + META, LAT), BF16, 0), ((GB * BLK, LAT), BF16, 0)],
        flops=2 * 512**3,
    )
    p = [p0] + [first(p0, k) for k in (1, 2, 3)]

    neighbours, cot_late, p0_late = lax.optimization_barrier((neighbours, cot, p0))
    here = band * NZ + patch
    off = jnp.mod(neighbours // MESH - here + 1, NX * NY * NZ)
    local = jnp.mod(neighbours, MESH)
    code = off * MESH + local
    code_row = jnp.pad(code.T, ((0, 2), (0, 0)))

    def side(which):
        rows = jnp.where(off == which, local, 300).astype(BF16).T
        rows = jnp.pad(rows, ((0, META - K), (0, LAT - MESH)))
        return jnp.concatenate([cot_late, rows], axis=0)

    ring = NX * NY * NZ
    up = [(i, (i + 1) % ring) for i in range(ring)]
    down = [((i + 1) % ring, i) for i in range(ring)]
    cp = lax.ppermute(side(2), ("band", "patch"), up)
    cn = lax.ppermute(side(0), ("band", "patch"), down)
    gs = call(
        cot_tables,
        [(cot, 0), (cp, 0), (cn, 0), (w[6], 0)],
        [((3 * MESH, LAT), F32, 0)],
        flops=6 * 256 * 512 * 512,
    )[0]

    mesh_bf = ((MESH, LAT), BF16, 0)
    mesh_f = ((MESH, LAT), F32, 0)
    q0, q1, q2, q3, table = call(
        route_sum,
        [(pos, 1)] + [(v, 0) for v in p],
        [mesh_f, mesh_bf, mesh_bf, mesh_bf, ((16,), I32, 1)],
        scratch=[pltpu.VMEM((8, BLK, LAT), F32)],
        flops=2 * 512**3,
    )
    got = [second(q, k) for k, q in ((1, q1), (2, q2), (3, q3))]
    ah, agg, sq, slope2, lat = call(
        mesh_forward,
        [(v, 0) for v in (q0, *got, ml, w[1], w[2], w[3])],
        [mesh_bf] * 5,
        flops=6 * 256 * 512 * 512,
    )
    lp = lax.ppermute(lat, ("band", "patch"), up)
    ln = lax.ppermute(lat, ("band", "patch"), down)
    snd, rcv = call(
        own_tables, [(v, 0) for v in (lat, w[4], w[5])], [mesh_bf, mesh_f], flops=4 * 256 * 512 * 512
    )
    summed, gsend, grecv, gl, gsec, ga, gm = call(
        edges_backward,
        [
            (v, 0)
            for v in (
                lp, ln, snd, rcv, code, code_row, cp, cn, gs, cot, slope2, w[1], w[2], w[3], w[4], w[5],
            )
        ],
        [mesh_bf] * 7,
        scratch=[
            pltpu.VMEM((3 * MESH, LAT), BF16),
            pltpu.VMEM((2 * MESH, LAT), F32),
            pltpu.VMEM((MESH, META), F32),
            pltpu.VMEM((K * MESH, LAT), BF16),
            pltpu.VMEM((MESH, LAT), F32),
        ],
        flops=5 * 10**9,
    )
    g = [gm] + [second(gm, k) for k in (1, 2, 3)]

    keep, give = call(
        mesh_weights,
        [(pos, 1)] + [(v, 0) for v in (ah, agg, sq, lat, summed, ga, gsec, gl, gsend, grecv, cot)],
        [((8, 768, 128), BF16, 0)] * 2,
        flops=12 * 256 * 512 * 512,
    )
    other = lax.ppermute(give, "rep", [(0, 1), (1, 0)])
    both = (keep.astype(F32) + other.astype(F32)).astype(BF16)
    zparts = lax.all_to_all(both, "patch", split_axis=0, concat_axis=0, tiled=True)

    r = call(
        return_pick,
        [(pos, 1), (table, 1)] + [(v, 0) for v in g],
        [((GB * BLK, LAT), BF16, 0)] * 4,
        flops=2 * 512**3,
    )
    rr = [r[0]] + [first(r[k], k) for k in (1, 2, 3)]
    gf, part1 = call(
        grid_backward,
        [(pos, 1), (codes, 1)] + [(v, 0) for v in (*rr, x, slot, slope1)],
        [((GB * BLK, LAT), BF16, 0), ((16, 128, 128), BF16, 0)],
        scratch=[pltpu.VMEM((GB * BLK, LAT), BF16)],
        flops=4 * 512**3,
    )
    mesh_part = call(z_sum, [(zparts, 0)], [((768, 128), BF16, 0)], flops=10**6)[0]
    mine = jnp.concatenate([part1, mesh_part.reshape(16, 48, 128)], axis=1)
    over_band = lax.all_to_all(mine, "band", split_axis=0, concat_axis=0, tiled=True)
    spread = call(band_sum, [(over_band, 0)], [((16, 176, 128), BF16, 0)], flops=10**6)[0]
    final = lax.all_to_all(spread, ("patch", "rep"), split_axis=0, concat_axis=0, tiled=True)
    grid_grad = call(
        grid_output, [(gf, 0), (w[0], 0)], [((GB * BLK, LAT), BF16, 0)], flops=2 * 512**3
    )[0]

    def last(parts, out):
        finish(parts, out, grid_scale=grid_scale, mesh_scale=mesh_scale)

    weight_part = call(last, [(final, 0)], [((7, 32, LAT), F32, 0)], flops=10**6)[0]
    return (grid_grad[None], gl[None], weight_part)


def solution(mesh):
    return jax.shard_map(
        body,
        mesh=mesh,
        in_specs=(
            P("rep", ("band", "patch"), None),
            P("rep", ("band", "patch"), None),
            P(),
            P(("band", "patch"), None),
            P(("band", "patch")),
            P(("band", "patch")),
            P(("band", "patch"), None),
            P("rep", ("band", "patch"), None),
        ),
        out_specs=(
            P("rep", ("band", "patch"), None),
            P("rep", ("band", "patch"), None),
            P(None, "band", None),
        ),
        check_vma=False,
    )
```

```python
import math

import jax
import jax.numpy as jnp
from jax import lax
from jax.experimental import pallas as pl
from jax.experimental.pallas import tpu as pltpu
from jax.sharding import PartitionSpec as P

F32 = jnp.float32
BF16 = jnp.bfloat16
I32 = jnp.int32
ALL = ("band", "patch", "rep")
NX, NY, NZ, NR = 4, 4, 8, 2
LAT = 512
BLK = 128
GB = 4
MESH = 256
K = 6
META = 16
RETURN_FLOPS = 25 * 10**9
VMEM = pl.BlockSpec(memory_space=pltpu.VMEM)
SMEM = pl.BlockSpec(memory_space=pltpu.SMEM)
FIRST = pl.BlockSpec((1, 512, 512), lambda i: (0, 0, 0), memory_space=pltpu.VMEM)


def nn(a, b):
    return lax.dot_general(a, b, (((1,), (0,)), ((), ())), preferred_element_type=F32)


def nt(a, b):
    return lax.dot_general(a, b, (((1,), (1,)), ((), ())), preferred_element_type=F32)


def tn(a, b):
    return lax.dot_general(a, b, (((0,), (0,)), ((), ())), preferred_element_type=F32)


def sigmoid(v):
    return 0.5 * jnp.tanh(0.5 * v) + 0.5


def call(kernel, ins, outs, scratch=(), flops=0, limit=8, **more):
    specs_in = [(VMEM, SMEM, FIRST)[s] for _, s in ins]
    out_shape = [jax.ShapeDtypeStruct(shape, dtype) for shape, dtype, _ in outs]
    specs_out = [SMEM if s else VMEM for _, _, s in outs]
    return pl.pallas_call(
        kernel,
        out_shape=out_shape,
        in_specs=specs_in,
        out_specs=specs_out,
        scratch_shapes=list(scratch),
        compiler_params=pltpu.CompilerParams(vmem_limit_bytes=limit * 1024 * 1024),
        cost_estimate=pl.CostEstimate(flops=flops, bytes_accessed=1000000, transcendentals=0),
        **more,
    )(*[a for a, _ in ins])


def device(x, y, z, r):
    return ((x * NY + y) * NZ + z) * NR + r


def shifts(k, flip):
    pairs = []
    for x in range(NX):
        for y in range(NY):
            for z in range(NZ):
                for r in range(NR):
                    along_x = (r == 0) != flip
                    to = device((x + k) % NX, y, z, r) if along_x else device(x, (y + k) % NY, z, r)
                    pairs.append((device(x, y, z, r), to))
    return pairs


def first(v, k):
    return lax.ppermute(v, ALL, shifts(k, False))


def second(v, k):
    return lax.ppermute(v, ALL, shifts(k, True))


def split_code(code, rep):
    t = lax.shift_right_logical(code, 1)
    tx = lax.shift_right_logical(t, 2)
    ty = t & 3
    d1 = jnp.where(rep == 0, tx, ty)
    d2 = jnp.where(rep == 0, ty, tx)
    return d1, d2, code & 1


def place(pos):
    v = pos[0]
    return v & 3, lax.shift_right_logical(v, 2) & 3, lax.shift_right_logical(v, 4) & 1, lax.shift_right_logical(v, 5)


def grid_forward(tb, tk, x, w, slot, out, slope):
    row = lax.broadcasted_iota(I32, (BLK, BLK), 0)
    for g in range(GB):
        rows = pl.ds(g * BLK, BLK)
        v = nn(x[rows, :], w[0])
        sg = sigmoid(v)
        h = v * sg
        slope[rows, :] = (sg + h * (1.0 - sg)).astype(BF16)
        pick = jnp.where(row == slot[g : g + 1, :], 1.0, 0.0).astype(BF16)
        out[rows, :] = nn(pick, h.astype(BF16)).astype(BF16)
    meta_row = lax.broadcasted_iota(I32, (META, LAT), 0)
    meta = jnp.zeros((META, LAT), F32)
    for g in range(GB):
        meta = jnp.where(meta_row == g, (tb[g] * 2 + tk[g]).astype(F32), meta)
    out[pl.ds(GB * BLK, META), :] = meta.astype(BF16)


def edge_codes(pos, near, row, col, up, down):
    local = (near[...] & (MESH - 1)).astype(F32)
    off = (lax.shift_right_logical(near[...], 8) - place(pos)[3] + 1) & (NX * NY * NZ - 1)
    code = off.astype(F32) * MESH + local
    full = jnp.concatenate([code, jnp.zeros((META - K, MESH), F32)], axis=0)
    row[...] = full
    col[...] = jnp.transpose(full)
    for out, which in ((up, 2), (down, 0)):
        ends = jnp.where(off == which, local, 300.0)
        ends = jnp.concatenate([ends, jnp.full((META - K, MESH), 300.0, F32)], axis=0)
        out[...] = jnp.concatenate([ends, ends], axis=1).astype(BF16)


def route_sum(pos, p0, p1, p2, p3, q0, q1, q2, q3, table, acc):
    own1, own2, rep, _ = place(pos)
    sources = (p0, p1, p2, p3)
    codes = []
    for p in sources:
        meta = p[pl.ds(GB * BLK, META), 0:128].astype(F32)
        codes += [jnp.max(meta[i : i + 1, :]).astype(I32) for i in range(GB)]
    acc[...] = jnp.zeros_like(acc)
    for n, code in enumerate(codes):
        table[n] = code
        d1, d2, blk = split_code(code, rep)
        slot = ((d2 - own2) & 3) * 2 + blk
        p, i = sources[n // GB], n % GB

        @pl.when(d1 == own1)
        def _():
            acc[slot] += p[pl.ds(i * BLK, BLK), :].astype(F32)

    for k, q in enumerate((q0, q1, q2, q3)):
        for b in range(2):
            q[pl.ds(b * BLK, BLK), :] = acc[2 * k + b].astype(q.dtype)


def mesh_forward(q0, r1, r2, r3, ml, w, up, down, ah, agg, sq, slope, lat_up, lat_down):
    total = q0[...] + r1[...].astype(F32) + r2[...].astype(F32) + r3[...].astype(F32)
    ah[...] = total.astype(BF16)
    agg[...] = nn(ah[...], w[1]).astype(BF16)
    v = nn(agg[...], w[2])
    sg = sigmoid(v)
    s = v * sg
    slope[...] = (sg + s * (1.0 - sg)).astype(BF16)
    sq[...] = s.astype(BF16)
    lat = (ml[...].astype(F32) + nn(sq[...], w[3])).astype(BF16)
    for out, ends in ((lat_up, up), (lat_down, down)):
        out[pl.ds(0, MESH), :] = lat
        out[pl.ds(MESH, META), :] = ends[...]


def own_tables(lat, w, snd, rcv):
    rows = lat[pl.ds(0, MESH), :]
    snd[...] = (nn(rows, w[4]) * 0.5).astype(BF16)
    rcv[...] = nn(rows, w[5]) * 0.5


def cot_tables(cot, cp, cn, w, gs):
    for j, c in enumerate((cp, cot, cn)):
        gs[pl.ds(j * MESH, MESH), :] = nt(c[...], w[6]) * 0.5


def edges_backward(
    lp, ln, snd, rcv, col, row, gs, cot, slope2, w,
    summed_b, gsend_b, grecv_b, gl_b, gsec_b, ga_b, gm_b, gl_out, gm_own,
    table, srcv, ecol, e, gsend,
):
    table[pl.ds(MESH, MESH), :] = snd[...]
    for j, c in enumerate((lp, ln)):
        rows = c[pl.ds(0, MESH), :]
        table[pl.ds(2 * j * MESH, MESH), :] = (nn(rows, w[4]) * 0.5).astype(BF16)
        srcv[pl.ds(j * MESH, MESH), :] = nn(rows, w[5]) * 0.5
    half = 128
    lane = lax.broadcasted_iota(I32, (half, 3 * MESH), 1).astype(F32)
    for m in range(2):
        rows = pl.ds(m * half, half)
        total = jnp.zeros((half, LAT), F32)
        recv = jnp.zeros((half, LAT), F32)
        for k in range(K):
            pick = jnp.where(lane == col[rows, k : k + 1], 1.0, 0.0).astype(BF16)
            h = nn(pick, table[...]) + rcv[rows, :]
            t = jnp.tanh(h)
            u = 1.0 + t
            s = h * u
            total = total + s
            eg = (gs[pl.ds(MESH + m * half, half), :] * (u + s * (1.0 - t))).astype(BF16)
            recv = recv + eg.astype(F32)
            e[pl.ds(k * MESH + m * half, half), :] = eg
        summed_b[rows, :] = total.astype(BF16)
        grecv_b[rows, :] = recv.astype(BF16)
    own = lax.broadcasted_iota(I32, (MESH, MESH), 0).astype(F32)
    acc = jnp.zeros((MESH, LAT), F32)
    for k in range(K):
        pick = jnp.where(own + float(MESH) == row[k : k + 1, :], 1.0, 0.0).astype(BF16)
        acc = acc + nn(pick, e[pl.ds(k * MESH, MESH), :])
    gsend[...] = acc
    lane2 = lax.broadcasted_iota(I32, (half, MESH), 1).astype(F32)
    for side, c in enumerate((lp, ln)):
        codes = c[pl.ds(MESH, META), 0:MESH].astype(F32)
        ecol[...] = jnp.transpose(codes)
        for k in range(K):
            for m in range(2):
                rows = pl.ds(m * half, half)
                pick = jnp.where(lane2 == ecol[rows, k : k + 1], 1.0, 0.0).astype(BF16)
                h = nn(pick, table[pl.ds(MESH, MESH), :]) + srcv[pl.ds(side * MESH + m * half, half), :]
                t = jnp.tanh(h)
                u = 1.0 + t
                g = gs[pl.ds(2 * side * MESH + m * half, half), :]
                e[pl.ds(k * MESH + m * half, half), :] = (g * (u + h * u * (1.0 - t))).astype(BF16)
        acc = gsend[...]
        for k in range(K):
            pick = jnp.where(own == codes[k : k + 1, :], 1.0, 0.0).astype(BF16)
            acc = acc + nn(pick, e[pl.ds(k * MESH, MESH), :])
        gsend[...] = acc
    gsend_b[...] = gsend[...].astype(BF16)
    gl = cot[...].astype(F32) + nt(gsend_b[...], w[4]) + nt(grecv_b[...], w[5])
    gl_b[...] = gl.astype(BF16)
    gl_out[...] = gl_b[...]
    gsec_b[...] = (nt(gl_b[...], w[3]) * slope2[...].astype(F32)).astype(BF16)
    ga_b[...] = nt(gsec_b[...], w[2]).astype(BF16)
    gm_b[...] = nt(ga_b[...], w[1]).astype(BF16)
    gm_own[...] = gm_b[...]


ZROWS = 512
BROWS = 224


def mesh_weights(pos, ah, agg, sq, lat, summed, ga, gsec, gl, gsend, grecv, cot, keep, give):
    rep = place(pos)[2]
    pairs = ((ah, ga), (agg, gsec), (sq, gl), (lat, gsend), (lat, grecv), (summed, cot))
    for out, h in ((give, 1 - rep), (keep, rep)):
        cols = pl.ds(pl.multiple_of(h * 256, 256), 256)
        for w, (left, right) in enumerate(pairs):
            part = tn(left[pl.ds(0, MESH), :], right[:, cols]).astype(BF16)
            for c in range(2):
                for b in range(16):
                    if w < 2:
                        at = NZ * ZROWS + b * 128 + w * 64 + c * 32
                    else:
                        at = (c * 4 + w - 2) * ZROWS + b * 32
                    out[pl.ds(at, 32), :] = part[b * 32 : b * 32 + 32, c * 128 : c * 128 + 128]


def pair_sum(a, b, out, moved):
    for dst, base in ((out, 0), (moved, NZ * ZROWS)):

        @pl.loop(0, dst.shape[0], step=64)
        def _(at):
            at = pl.multiple_of(at, 64)
            rows = pl.ds(base + at, 64)
            dst[pl.ds(at, 64), :] = (a[rows, :].astype(F32) + b[rows, :].astype(F32)).astype(BF16)


def return_pick(pos, table, g0, g1, g2, g3, r0, r1, r2, r3):
    own1, own2, rep, _ = place(pos)
    sources = (g0, g1, g2, g3)
    for k, r in enumerate((r0, r1, r2, r3)):
        j = (4 - k) % 4
        for i in range(GB):
            d1, d2, blk = split_code(table[j * GB + i], rep)
            at = (own2 - d2) & 3
            for n in range(4):

                @pl.when((d1 == own1) & (at == n))
                def _():
                    start = pl.multiple_of(blk * BLK, BLK)
                    r[pl.ds(i * BLK, BLK), :] = sources[n][pl.ds(start, BLK), :]


def grid_backward(pos, tb, r0, r1, r2, r3, x, slot, slope, gf, keep, give, picked):
    own1, _, rep, _ = place(pos)
    row = lax.broadcasted_iota(I32, (BLK, BLK), 0)
    for i in range(GB):
        d1, _, _ = split_code(tb[i] * 2, rep)
        at = (own1 - d1) & 3
        rows = pl.ds(i * BLK, BLK)
        for n, r in enumerate((r0, r1, r2, r3)):

            @pl.when(at == n)
            def _():
                picked[rows, :] = r[rows, :]

    for i in range(GB):
        rows = pl.ds(i * BLK, BLK)
        pick = jnp.where(row == slot[i : i + 1, :], 1.0, 0.0).astype(BF16)
        gf[rows, :] = (tn(pick, picked[rows, :]) * slope[rows, :].astype(F32)).astype(BF16)
    for out, h in ((give, 1 - rep), (keep, rep)):
        cols = pl.ds(pl.multiple_of(h * 256, 256), 256)
        part = tn(x[...], gf[:, cols]).astype(BF16)
        for b in range(16):
            for c in range(2):
                out[b, pl.ds(c * 32, 32), :] = part[b * 32 : b * 32 + 32, c * 128 : c * 128 + 128]


def grid_output(gf, w, out):
    out[...] = nt(gf[...], w[0]).astype(BF16)


def first_input(pos, keep, other, moved, zparts, *outs):
    own1, own2, rep, _ = place(pos)
    for k, out in enumerate(outs):
        for j in range(4):
            d, e = (own1 + k) & 3, (own2 + j) & 3
            b = jnp.where(rep == 0, d * 4 + e, e * 4 + d)
            out[pl.ds(j * BROWS, 64), :] = (keep[b].astype(F32) + other[b].astype(F32)).astype(BF16)
            rows = pl.ds(pl.multiple_of(b * 128, 128), 128)
            out[pl.ds(j * BROWS + 64, 128), :] = moved[rows, :]
            rows = pl.ds(pl.multiple_of(b * 32, 32), 32)
            total = zparts[0, rows, :].astype(F32)
            for z in range(1, NZ):
                total = total + zparts[z, rows, :].astype(F32)
            out[pl.ds(j * BROWS + 192, 32), :] = total.astype(BF16)


def first_sum(a, b, c, d, *outs):
    for j, out in enumerate(outs):
        rows = pl.ds(j * BROWS, BROWS)
        total = a[rows, :].astype(F32) + b[rows, :].astype(F32)
        out[...] = (total + c[rows, :].astype(F32) + d[rows, :].astype(F32)).astype(BF16)


def band_sum(a, b, c, d, out):
    total = a[...].astype(F32) + b[...].astype(F32) + c[...].astype(F32) + d[...].astype(F32)
    done = total.astype(BF16)
    for j in range(NZ):
        out[j] = done


def z_collect(parts, out):
    total = parts[0, 0:192, :].astype(F32)
    for j in range(1, NZ):
        total = total + parts[j, 0:192, :].astype(F32)
    out[pl.ds(0, 192), :] = total.astype(BF16)
    for j in range(NZ):
        out[pl.ds(192 + 32 * j, 32), :] = parts[j, 192:224, :]


def finish(pos, mine, other, out, *, grid_scale, mesh_scale):
    rep = place(pos)[2]
    for src, h in ((mine, rep), (other, 1 - rep)):
        for c in range(2):
            cols = pl.ds(pl.multiple_of(h * 256 + c * 128, 128), 128)
            for w in range(7):
                at = w * 64 + c * 32 if w < 3 else 192 + 32 * (c * 4 + w - 3)
                scale = grid_scale if w < 2 else mesh_scale
                out[w, :, cols] = src[pl.ds(at, 32), :].astype(F32) * scale


def body(
    grid_latents, mesh_latents, weights, target_band, target_block, node_slot, neighbours, mesh_cotangent
):
    grid_scale = 1.0 / math.sqrt(NR * GB * BLK * NX * NY * NZ)
    mesh_scale = 1.0 / math.sqrt(NR * MESH * NX * NY * NZ)
    band = lax.axis_index("band")
    patch = lax.axis_index("patch")
    rep = lax.axis_index("rep")
    bx, by = band >> 2, band & 3
    pos = jnp.where(rep == 0, bx | (by << 2), by | (bx << 2)) | (rep << 4) | ((band * NZ + patch) << 5)
    pos = pos.astype(I32).reshape(1)
    x = grid_latents[0]
    ml = mesh_latents[0]
    cot = mesh_cotangent[0]
    tb = target_band.reshape(GB)
    tk = target_block
    slot = node_slot.reshape(GB, BLK)
    ring = NX * NY * NZ
    up = [(i, (i + 1) % ring) for i in range(ring)]
    down = [((i + 1) % ring, i) for i in range(ring)]
    tie = lax.optimization_barrier

    cp = lax.ppermute(cot, ("band", "patch"), up)
    cn = lax.ppermute(cot, ("band", "patch"), down)
    p0, slope1 = call(
        grid_forward,
        [(tb, 1), (tk, 1), (x, 0), (weights, 2), (slot, 0)],
        [((GB * BLK + META, LAT), BF16, 0), ((GB * BLK, LAT), BF16, 0)],
        limit=60,
        grid=(1,),
        flops=2 * 512**3,
    )
    p = [p0] + [first(p0, k) for k in (1, 2, 3)]

    near, _ = tie((neighbours.T, p0))
    row, col, code_up, code_down = call(
        edge_codes,
        [(pos, 1), (near, 0)],
        [((META, MESH), F32, 0), ((MESH, META), F32, 0), ((META, LAT), BF16, 0), ((META, LAT), BF16, 0)],
        flops=10**6,
    )

    mesh_bf = ((MESH, LAT), BF16, 0)
    mesh_f = ((MESH, LAT), F32, 0)
    pay = ((MESH + META, LAT), BF16, 0)
    gs = call(
        cot_tables,
        [(cot, 0), (cp, 0), (cn, 0), (weights, 0)],
        [((3 * MESH, LAT), F32, 0)],
        flops=6 * 256 * 512 * 512,
    )[0]
    p[1], gs, row, col = tie((p[1], gs, row, col))
    q0, q1, q2, q3, table = call(
        route_sum,
        [(pos, 1)] + [(v, 0) for v in p],
        [mesh_f, mesh_bf, mesh_bf, mesh_bf, ((16,), I32, 1)],
        scratch=[pltpu.VMEM((8, BLK, LAT), F32)],
        flops=2 * 512**3,
    )
    got = [second(q, k) for k, q in ((1, q1), (2, q2), (3, q3))]
    ah, agg, sq, slope2, lat_up, lat_down = call(
        mesh_forward,
        [(v, 0) for v in (q0, *got, ml)] + [(weights, 0), (code_up, 0), (code_down, 0)],
        [mesh_bf] * 4 + [pay] * 2,
        flops=6 * 256 * 512 * 512,
    )
    lp = lax.ppermute(lat_up, ("band", "patch"), up)
    ln = lax.ppermute(lat_down, ("band", "patch"), down)
    snd, rcv = call(
        own_tables,
        [(lat_up, 0), (weights, 0)],
        [mesh_bf, mesh_f],
        flops=4 * 256 * 512 * 512
    )
    summed, gsend, grecv, gl, gsec, ga, gm, gl_out, gm_own = call(
        edges_backward,
        [(v, 0) for v in (lp, ln, snd, rcv, col, row, gs, cot, slope2)] + [(weights, 0)],
        [mesh_bf] * 9,
        scratch=[
            pltpu.VMEM((3 * MESH, LAT), BF16),
            pltpu.VMEM((2 * MESH, LAT), F32),
            pltpu.VMEM((MESH, META), F32),
            pltpu.VMEM((K * MESH, LAT), BF16),
            pltpu.VMEM((MESH, LAT), F32),
        ],
        flops=5 * 10**9,
        limit=16,
    )
    g = [gm_own] + [second(gm, k) for k in (1, 2, 3)]


    keep, give = call(
        mesh_weights,
        [(pos, 1)]
        + [(v, 0) for v in (ah, agg, sq, lat_up, summed, ga, gsec, gl, gsend, grecv, cot)],
        [((6144, 128), BF16, 0)] * 2,
        flops=12 * 256 * 512 * 512,
    )
    swap = [(0, 1), (1, 0)]
    other = lax.ppermute(give, "rep", swap)
    r = call(
        return_pick,
        [(pos, 1), (table, 1)] + [(v, 0) for v in g],
        [((GB * BLK, LAT), BF16, 0)] * 4,
        flops=RETURN_FLOPS,
    )
    rr = [r[0]] + [first(r[k], k) for k in (1, 2, 3)]
    both, moved = call(
        pair_sum,
        [(keep, 0), (other, 0)],
        [((NZ * ZROWS, 128), BF16, 0), ((2048, 128), BF16, 0)],
        flops=10**6,
    )
    zparts = lax.all_to_all(both, "patch", split_axis=0, concat_axis=0, tiled=True)
    zparts = zparts.reshape(NZ, ZROWS, 128)
    gf, keep1, give1 = call(
        grid_backward,
        [(pos, 1), (tb, 1)] + [(v, 0) for v in (*rr, x, slot, slope1)],
        [((GB * BLK, LAT), BF16, 0)] + [((16, 64, 128), BF16, 0)] * 2,
        scratch=[pltpu.VMEM((GB * BLK, LAT), BF16)],
        flops=4 * 512**3,
    )
    other1 = lax.ppermute(give1, "rep", swap)
    grid_grad = call(
        grid_output,
        [(gf, 0), (weights, 0)],
        [((GB * BLK, LAT), BF16, 0)],
        flops=2 * 512**3,
    )[0]
    keep1, grid_grad = tie((keep1, grid_grad))
    f = call(
        first_input,
        [(pos, 1)] + [(v, 0) for v in (keep1, other1, moved, zparts)],
        [((4 * BROWS, 128), BF16, 0)] * 4,
        flops=10**6,
    )
    f = [f[0]] + [first(f[k], k) for k in (1, 2, 3)]
    t = call(first_sum, [(v, 0) for v in f], [((BROWS, 128), BF16, 0)] * 4, flops=10**6)
    t = [t[0]] + [second(t[k], k) for k in (1, 2, 3)]
    spread = call(band_sum, [(v, 0) for v in t], [((NZ, BROWS, 128), BF16, 0)], flops=10**6)[0]
    over_z = lax.all_to_all(spread, "patch", split_axis=0, concat_axis=0, tiled=True)
    half_part = call(z_collect, [(over_z, 0)], [((448, 128), BF16, 0)], flops=10**6)[0]
    half_other = lax.ppermute(half_part, "rep", swap)

    def last(pos, mine, other, out):
        finish(pos, mine, other, out, grid_scale=grid_scale, mesh_scale=mesh_scale)

    weight_part = call(
        last, [(pos, 1), (half_part, 0), (half_other, 0)], [((7, 32, LAT), F32, 0)], flops=10**6
    )[0]
    return (grid_grad[None], gl_out[None], weight_part)


def solution(mesh):
    return jax.shard_map(
        body,
        mesh=mesh,
        in_specs=(
            P("rep", ("band", "patch"), None),
            P("rep", ("band", "patch"), None),
            P(),
            P(("band", "patch"), None),
            P(("band", "patch")),
            P(("band", "patch")),
            P(("band", "patch"), None),
            P("rep", ("band", "patch"), None),
        ),
        out_specs=(
            P("rep", ("band", "patch"), None),
            P("rep", ("band", "patch"), None),
            P(None, "band", None),
        ),
        check_vma=False,
    )
```

```python
import functools
import math

import jax
import jax.numpy as jnp
from jax import lax
from jax.experimental import pallas as pl
from jax.experimental.pallas import tpu as pltpu
from jax.sharding import PartitionSpec as P

F32 = jnp.float32
BF16 = jnp.bfloat16
I32 = jnp.int32
ALL = ("band", "patch", "rep")
NX, NY, NZ, NR = 4, 4, 8, 2
LAT = 512
BLK = 128
GB = 4
MESH = 256
K = 6
META = 16
RETURN_FLOPS = 25 * 10**9
VMEM = pl.BlockSpec(memory_space=pltpu.VMEM)
SMEM = pl.BlockSpec(memory_space=pltpu.SMEM)
FIRST = pl.BlockSpec((1, 512, 512), lambda i: (0, 0, 0), memory_space=pltpu.VMEM)


def nn(a, b):
    return lax.dot_general(a, b, (((1,), (0,)), ((), ())), preferred_element_type=F32)


def nt(a, b):
    return lax.dot_general(a, b, (((1,), (1,)), ((), ())), preferred_element_type=F32)


def tn(a, b):
    return lax.dot_general(a, b, (((0,), (0,)), ((), ())), preferred_element_type=F32)


def sigmoid(v):
    return 0.5 * jnp.tanh(0.5 * v) + 0.5


def call(kernel, ins, outs, scratch=(), flops=0, limit=8, **more):
    specs_in = [(VMEM, SMEM, FIRST)[s] for _, s in ins]
    out_shape = [jax.ShapeDtypeStruct(shape, dtype) for shape, dtype, _ in outs]
    specs_out = [SMEM if s else VMEM for _, _, s in outs]
    return pl.pallas_call(
        kernel,
        out_shape=out_shape,
        in_specs=specs_in,
        out_specs=specs_out,
        scratch_shapes=list(scratch),
        compiler_params=pltpu.CompilerParams(vmem_limit_bytes=limit * 1024 * 1024),
        cost_estimate=pl.CostEstimate(flops=flops, bytes_accessed=1000000, transcendentals=0),
        **more,
    )(*[a for a, _ in ins])


def device(x, y, z, r):
    return ((x * NY + y) * NZ + z) * NR + r


def shifts(k, flip):
    pairs = []
    for x in range(NX):
        for y in range(NY):
            for z in range(NZ):
                for r in range(NR):
                    along_x = (r == 0) != flip
                    to = device((x + k) % NX, y, z, r) if along_x else device(x, (y + k) % NY, z, r)
                    pairs.append((device(x, y, z, r), to))
    return pairs


def first(v, k):
    return lax.ppermute(v, ALL, shifts(k, False))


def second(v, k):
    return lax.ppermute(v, ALL, shifts(k, True))


def split_code(code, rep):
    t = lax.shift_right_logical(code, 1)
    tx = lax.shift_right_logical(t, 2)
    ty = t & 3
    d1 = jnp.where(rep == 0, tx, ty)
    d2 = jnp.where(rep == 0, ty, tx)
    return d1, d2, code & 1


def place(pos):
    v = pos[0]
    return v & 3, lax.shift_right_logical(v, 2) & 3, lax.shift_right_logical(v, 4) & 1, lax.shift_right_logical(v, 5)


def grid_forward(tb, tk, x, w, slot, out, slope):
    row = lax.broadcasted_iota(I32, (BLK, BLK), 0)
    for g in range(GB):
        rows = pl.ds(g * BLK, BLK)
        v = nn(x[rows, :], w[0])
        sg = sigmoid(v)
        h = v * sg
        slope[rows, :] = (sg + h * (1.0 - sg)).astype(BF16)
        pick = jnp.where(row == slot[g : g + 1, :], 1.0, 0.0).astype(BF16)
        out[rows, :] = nn(pick, h.astype(BF16)).astype(BF16)
    meta_row = lax.broadcasted_iota(I32, (META, LAT), 0)
    meta = jnp.zeros((META, LAT), F32)
    for g in range(GB):
        meta = jnp.where(meta_row == g, (tb[g] * 2 + tk[g]).astype(F32), meta)
    out[pl.ds(GB * BLK, META), :] = meta.astype(BF16)


def edge_codes(pos, near, row, col, up, down):
    local = (near[...] & (MESH - 1)).astype(F32)
    off = (lax.shift_right_logical(near[...], 8) - place(pos)[3] + 1) & (NX * NY * NZ - 1)
    code = off.astype(F32) * MESH + local
    full = jnp.concatenate([code, jnp.zeros((META - K, MESH), F32)], axis=0)
    row[...] = full
    col[...] = jnp.transpose(full)
    for out, which in ((up, 2), (down, 0)):
        ends = jnp.where(off == which, local, 300.0)
        ends = jnp.concatenate([ends, jnp.full((META - K, MESH), 300.0, F32)], axis=0)
        out[...] = jnp.concatenate([ends, ends], axis=1).astype(BF16)


def route_sum(pos, p0, p1, p2, p3, q0, q1, q2, q3, table, acc):
    own1, own2, rep, _ = place(pos)
    sources = (p0, p1, p2, p3)
    codes = []
    for p in sources:
        meta = p[pl.ds(GB * BLK, META), 0:128].astype(F32)
        codes += [jnp.max(meta[i : i + 1, :]).astype(I32) for i in range(GB)]
    acc[...] = jnp.zeros_like(acc)
    for n, code in enumerate(codes):
        table[n] = code
        d1, d2, blk = split_code(code, rep)
        slot = ((d2 - own2) & 3) * 2 + blk
        p, i = sources[n // GB], n % GB

        @pl.when(d1 == own1)
        def _():
            acc[slot] += p[pl.ds(i * BLK, BLK), :].astype(F32)

    for k, q in enumerate((q0, q1, q2, q3)):
        for b in range(2):
            q[pl.ds(b * BLK, BLK), :] = acc[2 * k + b].astype(q.dtype)


def mesh_forward(q0, r1, r2, r3, ml, w, up, down, ah, agg, sq, slope, lat_up, lat_down):
    total = q0[...] + r1[...].astype(F32) + r2[...].astype(F32) + r3[...].astype(F32)
    ah[...] = total.astype(BF16)
    agg[...] = nn(ah[...], w[1]).astype(BF16)
    v = nn(agg[...], w[2])
    sg = sigmoid(v)
    s = v * sg
    slope[...] = (sg + s * (1.0 - sg)).astype(BF16)
    sq[...] = s.astype(BF16)
    lat = (ml[...].astype(F32) + nn(sq[...], w[3])).astype(BF16)
    for out, ends in ((lat_up, up), (lat_down, down)):
        out[pl.ds(0, MESH), :] = lat
        out[pl.ds(MESH, META), :] = ends[...]


def cot_table(cot, w, gs):
    gs[...] = nt(cot[...], w[6]) * 0.5


def own_tables(lat, w, snd, rcv):
    rows = lat[pl.ds(0, MESH), :]
    snd[...] = (nn(rows, w[4]) * 0.5).astype(BF16)
    rcv[...] = nn(rows, w[5]) * 0.5


HALF = 128


def own_edges(lp, ln, snd, rcv, col, row, gs, w, summed_b, grecv_b, gsend, srcv, table, e):
    table[pl.ds(MESH, MESH), :] = snd[...]
    for j, c in enumerate((lp, ln)):
        rows = c[pl.ds(0, MESH), :]
        table[pl.ds(2 * j * MESH, MESH), :] = (nn(rows, w[4]) * 0.5).astype(BF16)
        srcv[pl.ds(j * MESH, MESH), :] = nn(rows, w[5]) * 0.5
    lane = lax.broadcasted_iota(I32, (HALF, 3 * MESH), 1).astype(F32)
    for m in range(2):
        rows = pl.ds(m * HALF, HALF)
        total = jnp.zeros((HALF, LAT), F32)
        recv = jnp.zeros((HALF, LAT), F32)
        for k in range(K):
            pick = jnp.where(lane == col[rows, k : k + 1], 1.0, 0.0).astype(BF16)
            h = nn(pick, table[...]) + rcv[rows, :]
            t = jnp.tanh(h)
            u = 1.0 + t
            s = h * u
            total = total + s
            eg = (gs[rows, :] * (u + s * (1.0 - t))).astype(BF16)
            recv = recv + eg.astype(F32)
            e[pl.ds(k * MESH + m * HALF, HALF), :] = eg
        summed_b[rows, :] = total.astype(BF16)
        grecv_b[rows, :] = recv.astype(BF16)
    own = lax.broadcasted_iota(I32, (MESH, MESH), 0).astype(F32)
    acc = jnp.zeros((MESH, LAT), F32)
    for k in range(K):
        pick = jnp.where(own + float(MESH) == row[k : k + 1, :], 1.0, 0.0).astype(BF16)
        acc = acc + nn(pick, e[pl.ds(k * MESH, MESH), :])
    gsend[...] = acc


def halo_edges(
    lp, ln, cp, cn, snd, srcv, gsend, grecv_b, cot, slope2, w,
    gsend_b, gl_b, gsec_b, ga_b, gm_b, gl_out, gm_own,
    ecol, e, gs, total,
):
    own = lax.broadcasted_iota(I32, (MESH, MESH), 0).astype(F32)
    lane = lax.broadcasted_iota(I32, (HALF, MESH), 1).astype(F32)
    total[...] = gsend[...]
    for side, (c, far) in enumerate(((lp, cp), (ln, cn))):
        gs[...] = nt(far[...], w[6]) * 0.5
        codes = c[pl.ds(MESH, META), 0:MESH].astype(F32)
        ecol[...] = jnp.transpose(codes)
        for k in range(K):
            for m in range(2):
                rows = pl.ds(m * HALF, HALF)
                pick = jnp.where(lane == ecol[rows, k : k + 1], 1.0, 0.0).astype(BF16)
                h = nn(pick, snd[...]) + srcv[pl.ds(side * MESH + m * HALF, HALF), :]
                t = jnp.tanh(h)
                u = 1.0 + t
                e[pl.ds(k * MESH + m * HALF, HALF), :] = (
                    gs[rows, :] * (u + h * u * (1.0 - t))
                ).astype(BF16)
        acc = total[...]
        for k in range(K):
            pick = jnp.where(own == codes[k : k + 1, :], 1.0, 0.0).astype(BF16)
            acc = acc + nn(pick, e[pl.ds(k * MESH, MESH), :])
        total[...] = acc
    gsend_b[...] = total[...].astype(BF16)
    gl = cot[...].astype(F32) + nt(gsend_b[...], w[4]) + nt(grecv_b[...], w[5])
    gl_b[...] = gl.astype(BF16)
    gl_out[...] = gl_b[...]
    gsec_b[...] = (nt(gl_b[...], w[3]) * slope2[...].astype(F32)).astype(BF16)
    ga_b[...] = nt(gsec_b[...], w[2]).astype(BF16)
    gm_b[...] = nt(ga_b[...], w[1]).astype(BF16)
    gm_own[...] = gm_b[...]


ZROWS = 512
BROWS = 224


def mesh_weights(pos, ah, agg, sq, lat, summed, ga, gsec, gl, gsend, grecv, cot, out, *, other):
    rep = place(pos)[2]
    h = 1 - rep if other else rep
    pairs = ((ah, ga), (agg, gsec), (sq, gl), (lat, gsend), (lat, grecv), (summed, cot))
    cols = pl.ds(pl.multiple_of(h * 256, 256), 256)
    for w, (left, right) in enumerate(pairs):
        part = tn(left[pl.ds(0, MESH), :], right[:, cols]).astype(BF16)
        for c in range(2):
            for b in range(16):
                if w < 2:
                    at = NZ * ZROWS + b * 128 + w * 64 + c * 32
                else:
                    at = (c * 4 + w - 2) * ZROWS + b * 32
                out[pl.ds(at, 32), :] = part[b * 32 : b * 32 + 32, c * 128 : c * 128 + 128]


def pair_sum(a, b, out, moved):
    for dst, base in ((out, 0), (moved, NZ * ZROWS)):

        @pl.loop(0, dst.shape[0], step=64)
        def _(at):
            at = pl.multiple_of(at, 64)
            rows = pl.ds(base + at, 64)
            dst[pl.ds(at, 64), :] = (a[rows, :].astype(F32) + b[rows, :].astype(F32)).astype(BF16)


def return_pick(pos, table, g0, g1, g2, g3, r0, r1, r2, r3):
    own1, own2, rep, _ = place(pos)
    sources = (g0, g1, g2, g3)
    for k, r in enumerate((r0, r1, r2, r3)):
        j = (4 - k) % 4
        for i in range(GB):
            d1, d2, blk = split_code(table[j * GB + i], rep)
            at = (own2 - d2) & 3
            for n in range(4):

                @pl.when((d1 == own1) & (at == n))
                def _():
                    start = pl.multiple_of(blk * BLK, BLK)
                    r[pl.ds(i * BLK, BLK), :] = sources[n][pl.ds(start, BLK), :]


def grid_backward(pos, tb, r0, r1, r2, r3, x, slot, slope, gf, keep, give, picked):
    own1, _, rep, _ = place(pos)
    row = lax.broadcasted_iota(I32, (BLK, BLK), 0)
    for i in range(GB):
        d1, _, _ = split_code(tb[i] * 2, rep)
        at = (own1 - d1) & 3
        rows = pl.ds(i * BLK, BLK)
        for n, r in enumerate((r0, r1, r2, r3)):

            @pl.when(at == n)
            def _():
                picked[rows, :] = r[rows, :]

    for i in range(GB):
        rows = pl.ds(i * BLK, BLK)
        pick = jnp.where(row == slot[i : i + 1, :], 1.0, 0.0).astype(BF16)
        gf[rows, :] = (tn(pick, picked[rows, :]) * slope[rows, :].astype(F32)).astype(BF16)
    for out, h in ((give, 1 - rep), (keep, rep)):
        cols = pl.ds(pl.multiple_of(h * 256, 256), 256)
        part = tn(x[...], gf[:, cols]).astype(BF16)
        for b in range(16):
            for c in range(2):
                out[b, pl.ds(c * 32, 32), :] = part[b * 32 : b * 32 + 32, c * 128 : c * 128 + 128]


def grid_output(gf, w, out):
    out[...] = nt(gf[...], w[0]).astype(BF16)


def first_input(pos, keep, other, moved, zparts, *outs):
    own1, own2, rep, _ = place(pos)
    for k, out in enumerate(outs):
        for j in range(4):
            d, e = (own1 + k) & 3, (own2 + j) & 3
            b = jnp.where(rep == 0, d * 4 + e, e * 4 + d)
            out[pl.ds(j * BROWS, 64), :] = (keep[b].astype(F32) + other[b].astype(F32)).astype(BF16)
            rows = pl.ds(pl.multiple_of(b * 128, 128), 128)
            out[pl.ds(j * BROWS + 64, 128), :] = moved[rows, :]
            rows = pl.ds(pl.multiple_of(b * 32, 32), 32)
            total = zparts[0, rows, :].astype(F32)
            for z in range(1, NZ):
                total = total + zparts[z, rows, :].astype(F32)
            out[pl.ds(j * BROWS + 192, 32), :] = total.astype(BF16)


def first_sum(a, b, c, d, *outs):
    for j, out in enumerate(outs):
        rows = pl.ds(j * BROWS, BROWS)
        total = a[rows, :].astype(F32) + b[rows, :].astype(F32)
        out[...] = (total + c[rows, :].astype(F32) + d[rows, :].astype(F32)).astype(BF16)


def band_sum(a, b, c, d, out):
    total = a[...].astype(F32) + b[...].astype(F32) + c[...].astype(F32) + d[...].astype(F32)
    done = total.astype(BF16)
    for j in range(NZ):
        out[j] = done


def z_collect(parts, out):
    total = parts[0, 0:192, :].astype(F32)
    for j in range(1, NZ):
        total = total + parts[j, 0:192, :].astype(F32)
    out[pl.ds(0, 192), :] = total.astype(BF16)
    for j in range(NZ):
        out[pl.ds(192 + 32 * j, 32), :] = parts[j, 192:224, :]


def finish(pos, mine, other, out, *, grid_scale, mesh_scale):
    rep = place(pos)[2]
    for src, h in ((mine, rep), (other, 1 - rep)):
        for c in range(2):
            cols = pl.ds(pl.multiple_of(h * 256 + c * 128, 128), 128)
            for w in range(7):
                at = w * 64 + c * 32 if w < 3 else 192 + 32 * (c * 4 + w - 3)
                scale = grid_scale if w < 2 else mesh_scale
                out[w, :, cols] = src[pl.ds(at, 32), :].astype(F32) * scale


def body(
    grid_latents, mesh_latents, weights, target_band, target_block, node_slot, neighbours, mesh_cotangent
):
    grid_scale = 1.0 / math.sqrt(NR * GB * BLK * NX * NY * NZ)
    mesh_scale = 1.0 / math.sqrt(NR * MESH * NX * NY * NZ)
    band = lax.axis_index("band")
    patch = lax.axis_index("patch")
    rep = lax.axis_index("rep")
    bx, by = band >> 2, band & 3
    pos = jnp.where(rep == 0, bx | (by << 2), by | (bx << 2)) | (rep << 4) | ((band * NZ + patch) << 5)
    pos = pos.astype(I32).reshape(1)
    x = grid_latents[0]
    ml = mesh_latents[0]
    cot = mesh_cotangent[0]
    tb = target_band.reshape(GB)
    tk = target_block
    slot = node_slot.reshape(GB, BLK)
    ring = NX * NY * NZ
    up = [(i, (i + 1) % ring) for i in range(ring)]
    down = [((i + 1) % ring, i) for i in range(ring)]
    tie = lax.optimization_barrier

    p0, slope1 = call(
        grid_forward,
        [(tb, 1), (tk, 1), (x, 0), (weights, 2), (slot, 0)],
        [((GB * BLK + META, LAT), BF16, 0), ((GB * BLK, LAT), BF16, 0)],
        limit=60,
        grid=(1,),
        flops=2 * 512**3,
    )
    p = [p0] + [first(p0, k) for k in (1, 2, 3)]

    near, _ = tie((neighbours.T, p0))
    row, col, code_up, code_down = call(
        edge_codes,
        [(pos, 1), (near, 0)],
        [((META, MESH), F32, 0), ((MESH, META), F32, 0), ((META, LAT), BF16, 0), ((META, LAT), BF16, 0)],
        flops=10**6,
    )

    mesh_bf = ((MESH, LAT), BF16, 0)
    mesh_f = ((MESH, LAT), F32, 0)
    pay = ((MESH + META, LAT), BF16, 0)
    near_cot, _ = tie((cot, p0))
    gs = call(cot_table, [(near_cot, 0), (weights, 0)], [mesh_f], flops=2 * 256 * 512 * 512)[0]
    p[1], gs, row, col = tie((p[1], gs, row, col))
    q0, q1, q2, q3, table = call(
        route_sum,
        [(pos, 1)] + [(v, 0) for v in p],
        [mesh_f, mesh_bf, mesh_bf, mesh_bf, ((16,), I32, 1)],
        scratch=[pltpu.VMEM((8, BLK, LAT), F32)],
        flops=2 * 512**3,
    )
    got = [second(q, k) for k, q in ((1, q1), (2, q2), (3, q3))]
    ah, agg, sq, slope2, lat_up, lat_down = call(
        mesh_forward,
        [(v, 0) for v in (q0, *got, ml)] + [(weights, 0), (code_up, 0), (code_down, 0)],
        [mesh_bf] * 4 + [pay] * 2,
        flops=6 * 256 * 512 * 512,
    )
    lp = lax.ppermute(lat_up, ("band", "patch"), up)
    ln = lax.ppermute(lat_down, ("band", "patch"), down)
    far, lat_down = tie((cot, lat_down))
    cp = lax.ppermute(far, ("band", "patch"), up)
    cn = lax.ppermute(far, ("band", "patch"), down)
    snd, rcv = call(
        own_tables,
        [(lat_up, 0), (weights, 0)],
        [mesh_bf, mesh_f],
        flops=4 * 256 * 512 * 512,
    )
    summed, grecv, gsend_own, srcv = call(
        own_edges,
        [(v, 0) for v in (lp, ln, snd, rcv, col, row, gs, weights)],
        [mesh_bf, mesh_bf, mesh_f, ((2 * MESH, LAT), F32, 0)],
        scratch=[pltpu.VMEM((3 * MESH, LAT), BF16), pltpu.VMEM((K * MESH, LAT), BF16)],
        flops=2 * 10**9,
        limit=12,
    )
    gsend, gl, gsec, ga, gm, gl_out, gm_own = call(
        halo_edges,
        [(v, 0) for v in (lp, ln, cp, cn, snd, srcv, gsend_own, grecv, cot, slope2, weights)],
        [mesh_bf] * 7,
        scratch=[
            pltpu.VMEM((MESH, META), F32),
            pltpu.VMEM((K * MESH, LAT), BF16),
            pltpu.VMEM((MESH, LAT), F32),
            pltpu.VMEM((MESH, LAT), F32),
        ],
        flops=3 * 10**9,
        limit=12,
    )
    g = [gm_own] + [second(gm, k) for k in (1, 2, 3)]


    give, keep = (
        call(
            functools.partial(mesh_weights, other=other),
            [(pos, 1)]
            + [(v, 0) for v in (ah, agg, sq, lat_up, summed, ga, gsec, gl, gsend, grecv, cot)],
            [((6144, 128), BF16, 0)],
            flops=6 * 256 * 512 * 512,
        )[0]
        for other in (True, False)
    )
    swap = [(0, 1), (1, 0)]
    other = lax.ppermute(give, "rep", swap)
    r = call(
        return_pick,
        [(pos, 1), (table, 1)] + [(v, 0) for v in g],
        [((GB * BLK, LAT), BF16, 0)] * 4,
        flops=RETURN_FLOPS,
    )
    rr = [r[0]] + [first(r[k], k) for k in (1, 2, 3)]
    both, moved = call(
        pair_sum,
        [(keep, 0), (other, 0)],
        [((NZ * ZROWS, 128), BF16, 0), ((2048, 128), BF16, 0)],
        flops=10**6,
    )
    zparts = lax.all_to_all(both, "patch", split_axis=0, concat_axis=0, tiled=True)
    zparts = zparts.reshape(NZ, ZROWS, 128)
    gf, keep1, give1 = call(
        grid_backward,
        [(pos, 1), (tb, 1)] + [(v, 0) for v in (*rr, x, slot, slope1)],
        [((GB * BLK, LAT), BF16, 0)] + [((16, 64, 128), BF16, 0)] * 2,
        scratch=[pltpu.VMEM((GB * BLK, LAT), BF16)],
        flops=4 * 512**3,
    )
    other1 = lax.ppermute(give1, "rep", swap)
    grid_grad = call(
        grid_output,
        [(gf, 0), (weights, 0)],
        [((GB * BLK, LAT), BF16, 0)],
        flops=2 * 512**3,
    )[0]
    keep1, grid_grad = tie((keep1, grid_grad))
    f = call(
        first_input,
        [(pos, 1)] + [(v, 0) for v in (keep1, other1, moved, zparts)],
        [((4 * BROWS, 128), BF16, 0)] * 4,
        flops=10**6,
    )
    f = [f[0]] + [first(f[k], k) for k in (1, 2, 3)]
    t = call(first_sum, [(v, 0) for v in f], [((BROWS, 128), BF16, 0)] * 4, flops=10**6)
    t = [t[0]] + [second(t[k], k) for k in (1, 2, 3)]
    spread = call(band_sum, [(v, 0) for v in t], [((NZ, BROWS, 128), BF16, 0)], flops=10**6)[0]
    over_z = lax.all_to_all(spread, "patch", split_axis=0, concat_axis=0, tiled=True)
    half_part = call(z_collect, [(over_z, 0)], [((448, 128), BF16, 0)], flops=10**6)[0]
    half_other = lax.ppermute(half_part, "rep", swap)

    def last(pos, mine, other, out):
        finish(pos, mine, other, out, grid_scale=grid_scale, mesh_scale=mesh_scale)

    weight_part = call(
        last, [(pos, 1), (half_part, 0), (half_other, 0)], [((7, 32, LAT), F32, 0)], flops=10**6
    )[0]
    return (grid_grad[None], gl_out[None], weight_part)


def solution(mesh):
    return jax.shard_map(
        body,
        mesh=mesh,
        in_specs=(
            P("rep", ("band", "patch"), None),
            P("rep", ("band", "patch"), None),
            P(),
            P(("band", "patch"), None),
            P(("band", "patch")),
            P(("band", "patch")),
            P(("band", "patch"), None),
            P("rep", ("band", "patch"), None),
        ),
        out_specs=(
            P("rep", ("band", "patch"), None),
            P("rep", ("band", "patch"), None),
            P(None, "band", None),
        ),
        check_vma=False,
    )
```

```python
import functools
import math

import jax
import jax.numpy as jnp
from jax import lax
from jax.experimental import pallas as pl
from jax.experimental.pallas import tpu as pltpu
from jax.sharding import PartitionSpec as P

F32 = jnp.float32
BF16 = jnp.bfloat16
I32 = jnp.int32
ALL = ("band", "patch", "rep")
NX, NY, NZ, NR = 4, 4, 8, 2
LAT = 512
BLK = 128
GB = 4
MESH = 256
K = 6
META = 16
RETURN_FLOPS = 25 * 10**9
VMEM = pl.BlockSpec(memory_space=pltpu.VMEM)
SMEM = pl.BlockSpec(memory_space=pltpu.SMEM)
FIRST = pl.BlockSpec((1, 512, 512), lambda i: (0, 0, 0), memory_space=pltpu.VMEM)


def nn(a, b):
    return lax.dot_general(a, b, (((1,), (0,)), ((), ())), preferred_element_type=F32)


def nt(a, b):
    return lax.dot_general(a, b, (((1,), (1,)), ((), ())), preferred_element_type=F32)


def tn(a, b):
    return lax.dot_general(a, b, (((0,), (0,)), ((), ())), preferred_element_type=F32)


def sigmoid(v):
    return 0.5 * jnp.tanh(0.5 * v) + 0.5


def call(kernel, ins, outs, scratch=(), flops=0, limit=8, **more):
    specs_in = [(VMEM, SMEM, FIRST)[s] for _, s in ins]
    out_shape = [jax.ShapeDtypeStruct(shape, dtype) for shape, dtype, _ in outs]
    specs_out = [SMEM if s else VMEM for _, _, s in outs]
    return pl.pallas_call(
        kernel,
        out_shape=out_shape,
        in_specs=specs_in,
        out_specs=specs_out,
        scratch_shapes=list(scratch),
        compiler_params=pltpu.CompilerParams(vmem_limit_bytes=limit * 1024 * 1024),
        cost_estimate=pl.CostEstimate(flops=flops, bytes_accessed=1000000, transcendentals=0),
        **more,
    )(*[a for a, _ in ins])


def device(x, y, z, r):
    return ((x * NY + y) * NZ + z) * NR + r


def shifts(k, flip):
    pairs = []
    for x in range(NX):
        for y in range(NY):
            for z in range(NZ):
                for r in range(NR):
                    along_x = (r == 0) != flip
                    to = device((x + k) % NX, y, z, r) if along_x else device(x, (y + k) % NY, z, r)
                    pairs.append((device(x, y, z, r), to))
    return pairs


def first(v, k):
    return lax.ppermute(v, ALL, shifts(k, False))


def second(v, k):
    return lax.ppermute(v, ALL, shifts(k, True))


def split_code(code, rep):
    t = lax.shift_right_logical(code, 1)
    tx = lax.shift_right_logical(t, 2)
    ty = t & 3
    d1 = jnp.where(rep == 0, tx, ty)
    d2 = jnp.where(rep == 0, ty, tx)
    return d1, d2, code & 1


def place(pos):
    v = pos[0]
    return v & 3, lax.shift_right_logical(v, 2) & 3, lax.shift_right_logical(v, 4) & 1, lax.shift_right_logical(v, 5)


def grid_forward(tb, tk, x, w, slot, out, slope):
    row = lax.broadcasted_iota(I32, (BLK, BLK), 0)
    for g in range(GB):
        rows = pl.ds(g * BLK, BLK)
        v = nn(x[rows, :], w[0])
        sg = sigmoid(v)
        h = v * sg
        slope[rows, :] = (sg + h * (1.0 - sg)).astype(BF16)
        pick = jnp.where(row == slot[g : g + 1, :], 1.0, 0.0).astype(BF16)
        out[rows, :] = nn(pick, h.astype(BF16)).astype(BF16)
    meta_row = lax.broadcasted_iota(I32, (META, LAT), 0)
    meta = jnp.zeros((META, LAT), F32)
    for g in range(GB):
        meta = jnp.where(meta_row == g, (tb[g] * 2 + tk[g]).astype(F32), meta)
    out[pl.ds(GB * BLK, META), :] = meta.astype(BF16)


def edge_codes(pos, near, row, col, up, down):
    local = (near[...] & (MESH - 1)).astype(F32)
    off = (lax.shift_right_logical(near[...], 8) - place(pos)[3] + 1) & (NX * NY * NZ - 1)
    code = off.astype(F32) * MESH + local
    full = jnp.concatenate([code, jnp.zeros((META - K, MESH), F32)], axis=0)
    row[...] = full
    col[...] = jnp.transpose(full)
    for out, which in ((up, 2), (down, 0)):
        ends = jnp.where(off == which, local, 300.0)
        ends = jnp.concatenate([ends, jnp.full((META - K, MESH), 300.0, F32)], axis=0)
        out[...] = jnp.concatenate([ends, ends], axis=1).astype(BF16)


def route_sum(pos, p0, p1, p2, p3, q0, q1, q2, q3, table, acc):
    own1, own2, rep, _ = place(pos)
    sources = (p0, p1, p2, p3)
    codes = []
    for p in sources:
        meta = p[pl.ds(GB * BLK, META), 0:128].astype(F32)
        codes += [jnp.max(meta[i : i + 1, :]).astype(I32) for i in range(GB)]
    acc[...] = jnp.zeros_like(acc)
    for n, code in enumerate(codes):
        table[n] = code
        d1, d2, blk = split_code(code, rep)
        slot = ((d2 - own2) & 3) * 2 + blk
        p, i = sources[n // GB], n % GB

        @pl.when(d1 == own1)
        def _():
            acc[slot] += p[pl.ds(i * BLK, BLK), :].astype(F32)

    for k, q in enumerate((q0, q1, q2, q3)):
        for b in range(2):
            q[pl.ds(b * BLK, BLK), :] = acc[2 * k + b].astype(q.dtype)


def mesh_forward(q0, r1, r2, r3, ml, w, up, down, ah, agg, sq, slope, lat_up, lat_down):
    total = q0[...] + r1[...].astype(F32) + r2[...].astype(F32) + r3[...].astype(F32)
    ah[...] = total.astype(BF16)
    agg[...] = nn(ah[...], w[1]).astype(BF16)
    v = nn(agg[...], w[2])
    sg = sigmoid(v)
    s = v * sg
    slope[...] = (sg + s * (1.0 - sg)).astype(BF16)
    sq[...] = s.astype(BF16)
    lat = (ml[...].astype(F32) + nn(sq[...], w[3])).astype(BF16)
    for out, ends in ((lat_up, up), (lat_down, down)):
        out[pl.ds(0, MESH), :] = lat
        out[pl.ds(MESH, META), :] = ends[...]


def cot_table(cot, w, gs):
    gs[...] = nt(cot[...], w[6]) * 0.5


def own_tables(lat, w, snd, rcv):
    rows = lat[pl.ds(0, MESH), :]
    snd[...] = (nn(rows, w[4]) * 0.5).astype(BF16)
    rcv[...] = nn(rows, w[5]) * 0.5


HALF = 128


def own_edges(lp, ln, snd, rcv, col, row, gs, w, summed_b, grecv_b, gsend, srcv, table, e):
    table[pl.ds(MESH, MESH), :] = snd[...]
    for j, c in enumerate((lp, ln)):
        rows = c[pl.ds(0, MESH), :]
        table[pl.ds(2 * j * MESH, MESH), :] = (nn(rows, w[4]) * 0.5).astype(BF16)
        srcv[pl.ds(j * MESH, MESH), :] = nn(rows, w[5]) * 0.5
    lane = lax.broadcasted_iota(I32, (HALF, 3 * MESH), 1).astype(F32)
    for m in range(2):
        rows = pl.ds(m * HALF, HALF)
        total = jnp.zeros((HALF, LAT), F32)
        recv = jnp.zeros((HALF, LAT), F32)
        for k in range(K):
            pick = jnp.where(lane == col[rows, k : k + 1], 1.0, 0.0).astype(BF16)
            h = nn(pick, table[...]) + rcv[rows, :]
            t = jnp.tanh(h)
            u = 1.0 + t
            s = h * u
            total = total + s
            eg = (gs[rows, :] * (u + s * (1.0 - t))).astype(BF16)
            recv = recv + eg.astype(F32)
            e[pl.ds(k * MESH + m * HALF, HALF), :] = eg
        summed_b[rows, :] = total.astype(BF16)
        grecv_b[rows, :] = recv.astype(BF16)
    own = lax.broadcasted_iota(I32, (MESH, MESH), 0).astype(F32)
    acc = jnp.zeros((MESH, LAT), F32)
    for k in range(K):
        pick = jnp.where(own + float(MESH) == row[k : k + 1, :], 1.0, 0.0).astype(BF16)
        acc = acc + nn(pick, e[pl.ds(k * MESH, MESH), :])
    gsend[...] = acc


def halo_edges(
    lp, ln, cp, cn, snd, srcv, gsend, grecv_b, cot, slope2, w,
    gsend_b, gl_b, gsec_b, ga_b, gm_b, gl_out, gm_own,
    ecol, e, gs, total,
):
    own = lax.broadcasted_iota(I32, (MESH, MESH), 0).astype(F32)
    lane = lax.broadcasted_iota(I32, (HALF, MESH), 1).astype(F32)
    total[...] = gsend[...]
    for side, (c, far) in enumerate(((lp, cp), (ln, cn))):
        gs[...] = nt(far[...], w[6]) * 0.5
        codes = c[pl.ds(MESH, META), 0:MESH].astype(F32)
        ecol[...] = jnp.transpose(codes)
        for k in range(K):
            for m in range(2):
                rows = pl.ds(m * HALF, HALF)
                pick = jnp.where(lane == ecol[rows, k : k + 1], 1.0, 0.0).astype(BF16)
                h = nn(pick, snd[...]) + srcv[pl.ds(side * MESH + m * HALF, HALF), :]
                t = jnp.tanh(h)
                u = 1.0 + t
                e[pl.ds(k * MESH + m * HALF, HALF), :] = (
                    gs[rows, :] * (u + h * u * (1.0 - t))
                ).astype(BF16)
        acc = total[...]
        for k in range(K):
            pick = jnp.where(own == codes[k : k + 1, :], 1.0, 0.0).astype(BF16)
            acc = acc + nn(pick, e[pl.ds(k * MESH, MESH), :])
        total[...] = acc
    gsend_b[...] = total[...].astype(BF16)
    gl = cot[...].astype(F32) + nt(gsend_b[...], w[4]) + nt(grecv_b[...], w[5])
    gl_b[...] = gl.astype(BF16)
    gl_out[...] = gl_b[...]
    gsec_b[...] = (nt(gl_b[...], w[3]) * slope2[...].astype(F32)).astype(BF16)
    ga_b[...] = nt(gsec_b[...], w[2]).astype(BF16)
    gm_b[...] = nt(ga_b[...], w[1]).astype(BF16)
    gm_own[...] = gm_b[...]


ZROWS = 512
BROWS = 224


def mesh_weights(pos, ah, agg, sq, lat, summed, ga, gsec, gl, gsend, grecv, cot, out, *, other):
    rep = place(pos)[2]
    h = 1 - rep if other else rep
    pairs = ((ah, ga), (agg, gsec), (sq, gl), (lat, gsend), (lat, grecv), (summed, cot))
    cols = pl.ds(pl.multiple_of(h * 256, 256), 256)
    for w, (left, right) in enumerate(pairs):
        part = tn(left[pl.ds(0, MESH), :], right[:, cols]).astype(BF16)
        for c in range(2):
            for b in range(16):
                if w < 2:
                    at = NZ * ZROWS + b * 128 + w * 64 + c * 32
                else:
                    at = (c * 4 + w - 2) * ZROWS + b * 32
                out[pl.ds(at, 32), :] = part[b * 32 : b * 32 + 32, c * 128 : c * 128 + 128]


def pair_sum(a, b, out, moved):
    for dst, base in ((out, 0), (moved, NZ * ZROWS)):

        @pl.loop(0, dst.shape[0], step=256)
        def _(at):
            at = pl.multiple_of(at, 256)
            rows = pl.ds(base + at, 256)
            dst[pl.ds(at, 256), :] = (a[rows, :].astype(F32) + b[rows, :].astype(F32)).astype(BF16)


def return_pick(pos, table, g0, g1, g2, g3, r0, r1, r2, r3):
    own1, own2, rep, _ = place(pos)
    sources = (g0, g1, g2, g3)
    for k, r in enumerate((r0, r1, r2, r3)):
        j = (4 - k) % 4
        for i in range(GB):
            d1, d2, blk = split_code(table[j * GB + i], rep)
            at = (own2 - d2) & 3
            for n in range(4):

                @pl.when((d1 == own1) & (at == n))
                def _():
                    start = pl.multiple_of(blk * BLK, BLK)
                    r[pl.ds(i * BLK, BLK), :] = sources[n][pl.ds(start, BLK), :]


def grid_backward(pos, tb, r0, r1, r2, r3, x, slot, slope, gf, keep, give, picked):
    own1, _, rep, _ = place(pos)
    row = lax.broadcasted_iota(I32, (BLK, BLK), 0)
    for i in range(GB):
        d1, _, _ = split_code(tb[i] * 2, rep)
        at = (own1 - d1) & 3
        rows = pl.ds(i * BLK, BLK)
        for n, r in enumerate((r0, r1, r2, r3)):

            @pl.when(at == n)
            def _():
                picked[rows, :] = r[rows, :]

    for i in range(GB):
        rows = pl.ds(i * BLK, BLK)
        pick = jnp.where(row == slot[i : i + 1, :], 1.0, 0.0).astype(BF16)
        gf[rows, :] = (tn(pick, picked[rows, :]) * slope[rows, :].astype(F32)).astype(BF16)
    for out, h in ((give, 1 - rep), (keep, rep)):
        cols = pl.ds(pl.multiple_of(h * 256, 256), 256)
        part = tn(x[...], gf[:, cols]).astype(BF16)
        for b in range(16):
            for c in range(2):
                out[b, pl.ds(c * 32, 32), :] = part[b * 32 : b * 32 + 32, c * 128 : c * 128 + 128]


def grid_output(gf, w, out):
    out[...] = nt(gf[...], w[0]).astype(BF16)


def first_input(pos, keep, other, moved, zparts, *outs):
    own1, own2, rep, _ = place(pos)
    for k, out in enumerate(outs):
        for j in range(4):
            d, e = (own1 + k) & 3, (own2 + j) & 3
            b = jnp.where(rep == 0, d * 4 + e, e * 4 + d)
            out[pl.ds(j * BROWS, 64), :] = (keep[b].astype(F32) + other[b].astype(F32)).astype(BF16)
            rows = pl.ds(pl.multiple_of(b * 128, 128), 128)
            out[pl.ds(j * BROWS + 64, 128), :] = moved[rows, :]
            rows = pl.ds(pl.multiple_of(b * 32, 32), 32)
            total = zparts[0, rows, :].astype(F32)
            for z in range(1, NZ):
                total = total + zparts[z, rows, :].astype(F32)
            out[pl.ds(j * BROWS + 192, 32), :] = total.astype(BF16)


def first_sum(a, b, c, d, *outs):
    for j, out in enumerate(outs):
        rows = pl.ds(j * BROWS, BROWS)
        total = a[rows, :].astype(F32) + b[rows, :].astype(F32)
        out[...] = (total + c[rows, :].astype(F32) + d[rows, :].astype(F32)).astype(BF16)


def band_sum(a, b, c, d, out):
    total = a[...].astype(F32) + b[...].astype(F32) + c[...].astype(F32) + d[...].astype(F32)
    done = total.astype(BF16)
    for j in range(NZ):
        out[j] = done


def z_collect(parts, out):
    total = parts[0, 0:192, :].astype(F32)
    for j in range(1, NZ):
        total = total + parts[j, 0:192, :].astype(F32)
    out[pl.ds(0, 192), :] = total.astype(BF16)
    for j in range(NZ):
        out[pl.ds(192 + 32 * j, 32), :] = parts[j, 192:224, :]


def finish(pos, mine, other, out, *, grid_scale, mesh_scale):
    rep = place(pos)[2]
    for src, h in ((mine, rep), (other, 1 - rep)):
        for c in range(2):
            cols = pl.ds(pl.multiple_of(h * 256 + c * 128, 128), 128)
            for w in range(7):
                at = w * 64 + c * 32 if w < 3 else 192 + 32 * (c * 4 + w - 3)
                scale = grid_scale if w < 2 else mesh_scale
                out[w, :, cols] = src[pl.ds(at, 32), :].astype(F32) * scale


def body(
    grid_latents, mesh_latents, weights, target_band, target_block, node_slot, neighbours, mesh_cotangent
):
    grid_scale = 1.0 / math.sqrt(NR * GB * BLK * NX * NY * NZ)
    mesh_scale = 1.0 / math.sqrt(NR * MESH * NX * NY * NZ)
    band = lax.axis_index("band")
    patch = lax.axis_index("patch")
    rep = lax.axis_index("rep")
    bx, by = band >> 2, band & 3
    pos = jnp.where(rep == 0, bx | (by << 2), by | (bx << 2)) | (rep << 4) | ((band * NZ + patch) << 5)
    pos = pos.astype(I32).reshape(1)
    x = grid_latents[0]
    ml = mesh_latents[0]
    cot = mesh_cotangent[0]
    tb = target_band.reshape(GB)
    tk = target_block
    slot = node_slot.reshape(GB, BLK)
    ring = NX * NY * NZ
    up = [(i, (i + 1) % ring) for i in range(ring)]
    down = [((i + 1) % ring, i) for i in range(ring)]
    tie = lax.optimization_barrier

    p0, slope1 = call(
        grid_forward,
        [(tb, 1), (tk, 1), (x, 0), (weights, 2), (slot, 0)],
        [((GB * BLK + META, LAT), BF16, 0), ((GB * BLK, LAT), BF16, 0)],
        limit=60,
        grid=(1,),
        flops=2 * 512**3,
    )
    p = [p0] + [first(p0, k) for k in (1, 2, 3)]

    near, _ = tie((neighbours.T, p0))
    row, col, code_up, code_down = call(
        edge_codes,
        [(pos, 1), (near, 0)],
        [((META, MESH), F32, 0), ((MESH, META), F32, 0), ((META, LAT), BF16, 0), ((META, LAT), BF16, 0)],
        flops=10**6,
    )

    mesh_bf = ((MESH, LAT), BF16, 0)
    mesh_f = ((MESH, LAT), F32, 0)
    pay = ((MESH + META, LAT), BF16, 0)
    near_cot, _ = tie((cot, p0))
    gs = call(cot_table, [(near_cot, 0), (weights, 0)], [mesh_f], flops=2 * 256 * 512 * 512)[0]
    p[1], gs, row, col = tie((p[1], gs, row, col))
    q0, q1, q2, q3, table = call(
        route_sum,
        [(pos, 1)] + [(v, 0) for v in p],
        [mesh_f, mesh_bf, mesh_bf, mesh_bf, ((16,), I32, 1)],
        scratch=[pltpu.VMEM((8, BLK, LAT), F32)],
        flops=2 * 512**3,
    )
    got = [second(q, k) for k, q in ((1, q1), (2, q2), (3, q3))]
    ah, agg, sq, slope2, lat_up, lat_down = call(
        mesh_forward,
        [(v, 0) for v in (q0, *got, ml)] + [(weights, 0), (code_up, 0), (code_down, 0)],
        [mesh_bf] * 4 + [pay] * 2,
        flops=6 * 256 * 512 * 512,
    )
    lp = lax.ppermute(lat_up, ("band", "patch"), up)
    ln = lax.ppermute(lat_down, ("band", "patch"), down)
    far, lat_down = tie((cot, lat_down))
    cp = lax.ppermute(far, ("band", "patch"), up)
    cn = lax.ppermute(far, ("band", "patch"), down)
    snd, rcv = call(
        own_tables,
        [(lat_up, 0), (weights, 0)],
        [mesh_bf, mesh_f],
        flops=4 * 256 * 512 * 512,
    )
    summed, grecv, gsend_own, srcv = call(
        own_edges,
        [(v, 0) for v in (lp, ln, snd, rcv, col, row, gs, weights)],
        [mesh_bf, mesh_bf, mesh_f, ((2 * MESH, LAT), F32, 0)],
        scratch=[pltpu.VMEM((3 * MESH, LAT), BF16), pltpu.VMEM((K * MESH, LAT), BF16)],
        flops=2 * 10**9,
        limit=12,
    )
    gsend, gl, gsec, ga, gm, gl_out, gm_own = call(
        halo_edges,
        [(v, 0) for v in (lp, ln, cp, cn, snd, srcv, gsend_own, grecv, cot, slope2, weights)],
        [mesh_bf] * 7,
        scratch=[
            pltpu.VMEM((MESH, META), F32),
            pltpu.VMEM((K * MESH, LAT), BF16),
            pltpu.VMEM((MESH, LAT), F32),
            pltpu.VMEM((MESH, LAT), F32),
        ],
        flops=3 * 10**9,
        limit=12,
    )
    g = [gm_own] + [second(gm, k) for k in (1, 2, 3)]


    give, keep = (
        call(
            functools.partial(mesh_weights, other=other),
            [(pos, 1)]
            + [(v, 0) for v in (ah, agg, sq, lat_up, summed, ga, gsec, gl, gsend, grecv, cot)],
            [((6144, 128), BF16, 0)],
            flops=6 * 256 * 512 * 512,
        )[0]
        for other in (True, False)
    )
    swap = [(0, 1), (1, 0)]
    other = lax.ppermute(give, "rep", swap)
    r = call(
        return_pick,
        [(pos, 1), (table, 1)] + [(v, 0) for v in g],
        [((GB * BLK, LAT), BF16, 0)] * 4,
        flops=RETURN_FLOPS,
    )
    rr = [r[0]] + [first(r[k], k) for k in (1, 2, 3)]
    both, moved = call(
        pair_sum,
        [(keep, 0), (other, 0)],
        [((NZ * ZROWS, 128), BF16, 0), ((2048, 128), BF16, 0)],
        flops=10**6,
    )
    zparts = lax.all_to_all(both, "patch", split_axis=0, concat_axis=0, tiled=True)
    zparts = zparts.reshape(NZ, ZROWS, 128)
    gf, keep1, give1 = call(
        grid_backward,
        [(pos, 1), (tb, 1)] + [(v, 0) for v in (*rr, x, slot, slope1)],
        [((GB * BLK, LAT), BF16, 0)] + [((16, 64, 128), BF16, 0)] * 2,
        scratch=[pltpu.VMEM((GB * BLK, LAT), BF16)],
        flops=4 * 512**3,
    )
    other1 = lax.ppermute(give1, "rep", swap)
    grid_grad = call(
        grid_output,
        [(gf, 0), (weights, 0)],
        [((GB * BLK, LAT), BF16, 0)],
        flops=2 * 512**3,
    )[0]
    keep1, grid_grad = tie((keep1, grid_grad))
    f = call(
        first_input,
        [(pos, 1)] + [(v, 0) for v in (keep1, other1, moved, zparts)],
        [((4 * BROWS, 128), BF16, 0)] * 4,
        flops=10**6,
    )
    f = [f[0]] + [first(f[k], k) for k in (1, 2, 3)]
    t = call(first_sum, [(v, 0) for v in f], [((BROWS, 128), BF16, 0)] * 4, flops=10**6)
    t = [t[0]] + [second(t[k], k) for k in (1, 2, 3)]
    spread = call(band_sum, [(v, 0) for v in t], [((NZ, BROWS, 128), BF16, 0)], flops=10**6)[0]
    over_z = lax.all_to_all(spread, "patch", split_axis=0, concat_axis=0, tiled=True)
    half_part = call(z_collect, [(over_z, 0)], [((448, 128), BF16, 0)], flops=10**6)[0]
    half_other = lax.ppermute(half_part, "rep", swap)

    def last(pos, mine, other, out):
        finish(pos, mine, other, out, grid_scale=grid_scale, mesh_scale=mesh_scale)

    weight_part = call(
        last, [(pos, 1), (half_part, 0), (half_other, 0)], [((7, 32, LAT), F32, 0)], flops=10**6
    )[0]
    return (grid_grad[None], gl_out[None], weight_part)


def solution(mesh):
    return jax.shard_map(
        body,
        mesh=mesh,
        in_specs=(
            P("rep", ("band", "patch"), None),
            P("rep", ("band", "patch"), None),
            P(),
            P(("band", "patch"), None),
            P(("band", "patch")),
            P(("band", "patch")),
            P(("band", "patch"), None),
            P("rep", ("band", "patch"), None),
        ),
        out_specs=(
            P("rep", ("band", "patch"), None),
            P("rep", ("band", "patch"), None),
            P(None, "band", None),
        ),
        check_vma=False,
    )
```
